32 devices in a mesh: segment: 2 (over core), expert: 16 (over z, y, x).
Axes of the slice: x: 2, y: 2, z: 4, core: 2. Of those that a mesh axis runs over, the one named last changes fastest.
Arguments:
- fwd_input: bfloat16 [2, 1024, 1024], P('segment', 'expert'), may hold values from -6 to 6
- fwd_routes: int32 [2, 1024, 8], P('segment', 'expert'), may hold values from 0 to 15, all different within a row; in each aligned block of 64 rows (0 to 63, 64 to 127, ..., all dimensions but the last counted through in order) at most 32 rows name the same one
- fwd_gates: float32 [2, 1024, 8], P('segment', 'expert'), may hold values from 0.05 to 0.3
- bwd_input: bfloat16 [2, 1024, 1024], P('segment', 'expert'), may hold values from -6 to 6
- bwd_grad: bfloat16 [2, 1024, 1024], P('segment', 'expert'), may hold values from -6 to 6
- bwd_routes: int32 [2, 1024, 8], P('segment', 'expert'), may hold values from 0 to 15, all different within a row; in each aligned block of 64 rows (0 to 63, 64 to 127, ..., all dimensions but the last counted through in order) at most 32 rows name the same one
- bwd_gates: float32 [2, 1024, 8], P('segment', 'expert'), may hold values from 0.05 to 0.3
- norm_gain: float32 [2, 1024], P('segment'), may hold values from 0.25 to 1.75
- w_gate: bfloat16 [2, 16, 1024, 768], P('segment', 'expert'), may hold values from -0.1875 to 0.1875
- w_up: bfloat16 [2, 16, 1024, 768], P('segment', 'expert'), may hold values from -0.1875 to 0.1875
- w_down: bfloat16 [2, 16, 768, 1024], P('segment', 'expert'), may hold values from -0.21875 to 0.21875
Outputs:
- fwd_out: bfloat16 [2, 1024, 1024], P('segment', 'expert')
- bwd_out: bfloat16 [2, 1024, 1024], P('segment', 'expert')
The draws below stay inside these ranges and needn't reach their ends.
Inputs may be any that keep to these rules, and one draw needn't show every extreme that they name: `fwd_routes`: each token names 8 different experts; within the 64 rows of one device (aligned blocks) no expert is named by more than 32 rows, a bound that some block reaches. `bwd_routes`: as for fwd_routes.
All inputs are finite; a program needn't handle non-finite values.
Results may differ from the reference program's by a relative error of at most 0.0051.
Values may be sent and summed in bfloat16 or wider, within the bound.
No kernel may reach another device: no remote copies, remote signals or barrier semaphores. Data moves between devices by JAX's collectives and lax.ppermute only.
A program may use at most 64 MiB of HBM per device.

```python
import math
import jax
import jax.numpy as jnp
import numpy as np
from jax import lax

D = 1024
FF = 768
TOP = 8
TOK_DEV = 64
EXPERTS = 16
LAYERS = 2
CAP = 32
TOKENS = 1024
N_EXPERT = 16


def shard_levels(own_key, shape, split, smallest, top_value):
    factor_of = 1.0
    for dim, shards_of in split:
        heights = jax.random.uniform(jax.random.fold_in(jax.random.fold_in(own_key, 6), dim), (shards_of,), jnp.float32, smallest / len(split), top_value / len(split))
        factor_of = factor_of * jnp.repeat(jnp.exp(heights), shape[dim] // shards_of).reshape((-1,) + (1,) * (len(shape) - 1 - dim))
    return factor_of


def assign_block(key, own, number, rows, amount, top, bound, slope):
    ranking = jax.random.permutation(key, amount)
    crowded, common = portions_of(amount, rows * top, bound, slope, True), portions_of(amount, rows * top, bound, slope, False)
    places = jnp.arange(amount)

    def named(sizes, offset_by):
        used = int((sizes > 0).sum())
        fixed = max(1, used // 4)
        shifted = fixed + (places - fixed + offset_by * (used - fixed)) % max(1, amount - fixed)
        return jnp.zeros((amount,), jnp.int32).at[ranking[jnp.where(places < fixed, places, shifted)]].set(jnp.asarray(sizes, jnp.int32))

    sizes = jnp.where(number % 4 == 0, named(crowded, number // 4), named(common, number - number // 4 - 1))
    mixed = jax.random.permutation(jax.random.fold_in(own, 3), amount)
    donor, taker = mixed[0:amount // 2 * 2:2], mixed[1:amount // 2 * 2:2]
    margin = jnp.minimum(sizes[donor] - 1, bound - sizes[taker]) // 2
    margin = jnp.where((donor == ranking[0]) | (taker == ranking[0]) | (sizes[taker] == 0), 0, jnp.maximum(margin, 0))
    shifted = jax.random.randint(jax.random.fold_in(own, 4), (amount // 2,), 0, 1 << 20) % (margin + 1)
    sizes = sizes.at[donor].add(-shifted).at[taker].add(shifted)
    labels = jnp.searchsorted(jnp.cumsum(sizes), jnp.arange(rows * top), side="right").astype(jnp.int32)
    table = labels.reshape(top, rows).T
    table = table[jax.random.permutation(jax.random.fold_in(own, 1), rows)]
    offset_by = jax.random.randint(jax.random.fold_in(own, 2), (rows, 1), 0, top)
    return jnp.take_along_axis(table, (jnp.arange(top)[None, :] + offset_by) % top, axis=1)


def portions_of(number_of, total, limit, skew, full):
    loads = [(1 << 20) // math.isqrt(rank ** skew) + 1 for rank in range(1, number_of + 1)]
    largest = limit if full else min(limit, max(-(-total // number_of), total * loads[0] // sum(loads)))
    least = 1 if total - largest >= number_of - 1 else 0
    given, surplus = [largest] + [least] * (number_of - 1), total - largest - least * (number_of - 1)
    while surplus > 0:
        movable = [i for i in range(1, number_of) if given[i] < largest] or [i for i in range(1, number_of) if given[i] < limit]
        whole, budget = sum([loads[i] for i in movable]), surplus
        for i in movable:
            extra = min(limit - given[i], max(1, budget * loads[i] // whole), surplus)
            given[i] = given[i] + extra
            surplus = surplus - extra
    return np.array(given)


def gaussian(key, shape, deviation, most, shards=(), kind=jnp.bfloat16):
    level = shard_levels(key, shape, shards, -0.22, 0.18) if shards else 1.0
    drawn = jax.random.normal(key, shape, jnp.float32) * deviation * level
    return jnp.minimum(jnp.maximum(drawn, -most), most).astype(kind)


def setup_inputs(seed: int = 0) -> dict:
    splits = jax.random.split(jax.random.key(seed), 12)
    fwd_input = gaussian(splits[0], (LAYERS, TOKENS, D), 1.0, 6.0, ((0, 2), (1, 16)))
    fwd_routes_keys = jax.random.split(jax.random.fold_in(splits[1], 1), LAYERS * TOKENS // TOK_DEV)
    fwd_routes_turns = jax.random.permutation(jax.random.fold_in(splits[1], 3), LAYERS * TOKENS // TOK_DEV)
    fwd_routes = jax.vmap(lambda own, number: assign_block(jax.random.fold_in(splits[1], 2), own, number, TOK_DEV, EXPERTS, TOP, CAP, 0))(fwd_routes_keys, fwd_routes_turns).reshape((LAYERS, TOKENS, TOP))
    fwd_gates = jnp.clip(0.05 + 0.25 * jax.random.uniform(splits[2], (LAYERS, TOKENS, TOP), jnp.float32) ** shard_levels(splits[2], (LAYERS, TOKENS, TOP), ((0, 2), (1, 16)), -0.2, 0.2), 0.05, 0.3)
    bwd_input = gaussian(splits[3], (LAYERS, TOKENS, D), 1.0, 6.0, ((0, 2), (1, 16)))
    bwd_grad = gaussian(splits[4], (LAYERS, TOKENS, D), 1.0, 6.0, ((0, 2), (1, 16)))
    bwd_routes_keys = jax.random.split(jax.random.fold_in(splits[5], 1), LAYERS * TOKENS // TOK_DEV)
    bwd_routes_turns = jax.random.permutation(jax.random.fold_in(splits[5], 3), LAYERS * TOKENS // TOK_DEV)
    bwd_routes = jax.vmap(lambda own, number: assign_block(jax.random.fold_in(splits[5], 2), own, number, TOK_DEV, EXPERTS, TOP, CAP, 0))(bwd_routes_keys, bwd_routes_turns).reshape((LAYERS, TOKENS, TOP))
    bwd_gates = jnp.clip(0.05 + 0.25 * jax.random.uniform(splits[6], (LAYERS, TOKENS, TOP), jnp.float32) ** shard_levels(splits[6], (LAYERS, TOKENS, TOP), ((0, 2), (1, 16)), -0.2, 0.2), 0.05, 0.3)
    norm_gain = jnp.clip(1.0 + 0.15 * jax.random.normal(splits[7], (LAYERS, D), jnp.float32), 0.25, 1.75)
    w_gate = gaussian(splits[8], (LAYERS, EXPERTS, D, FF), D ** -0.5, 0.1875, ((0, 2), (1, 16)))
    w_up = gaussian(splits[9], (LAYERS, EXPERTS, D, FF), D ** -0.5, 0.1875, ((0, 2), (1, 16)))
    w_down = gaussian(splits[10], (LAYERS, EXPERTS, FF, D), FF ** -0.5, 0.21875, ((0, 2), (1, 16)))
    return {"fwd_input": fwd_input, "fwd_routes": fwd_routes, "fwd_gates": fwd_gates, "bwd_input": bwd_input, "bwd_grad": bwd_grad, "bwd_routes": bwd_routes, "bwd_gates": bwd_gates, "norm_gain": norm_gain, "w_gate": w_gate, "w_up": w_up, "w_down": w_down}


EPSILON = 1e-06

def norm_scale(stream):
    return lax.rsqrt(lax.optimization_barrier(jnp.mean(stream * stream, axis=-1, keepdims=True)) + EPSILON)

def slot_index(routes):
    blocks = routes.reshape(N_EXPERT, TOK_DEV * TOP)
    onehot = (blocks[:, :, None] == jnp.arange(EXPERTS, dtype=jnp.int32)[None, None, :]).astype(jnp.int32)
    before = jnp.cumsum(onehot, axis=1) - onehot
    position = lax.optimization_barrier(jnp.sum(before * onehot, axis=2)).astype(jnp.int32)
    source = jnp.arange(N_EXPERT, dtype=jnp.int32)[:, None]
    return (blocks * (N_EXPERT * CAP) + source * CAP + position).reshape(-1).astype(jnp.int32)

def expert_forward(inputs, gate_matrix, up_matrix, down_matrix):
    gate = jnp.dot(inputs, gate_matrix, preferred_element_type=jnp.float32)
    upward = jnp.dot(inputs, up_matrix, preferred_element_type=jnp.float32)
    hidden = (gate * jax.nn.sigmoid(gate) * upward).astype(jnp.bfloat16)
    return jnp.dot(hidden, down_matrix, preferred_element_type=jnp.float32).astype(jnp.bfloat16)

def transposed(left, right):
    return lax.dot_general(left, right, (((1,), (1,)), ((), ())), preferred_element_type=jnp.float32)

def expert_backward(inputs, grads, gate_matrix, up_matrix, down_matrix):
    gate = jnp.dot(inputs, gate_matrix, preferred_element_type=jnp.float32)
    upward = jnp.dot(inputs, up_matrix, preferred_element_type=jnp.float32)
    d_hidden = transposed(grads, down_matrix)
    sigma = jax.nn.sigmoid(gate)
    d_gate = (d_hidden * upward * sigma * (1.0 + gate * (1.0 - sigma))).astype(jnp.bfloat16)
    d_up = (d_hidden * gate * sigma).astype(jnp.bfloat16)
    return (transposed(d_gate, gate_matrix) + transposed(d_up, up_matrix)).astype(jnp.bfloat16)

def to_buffer(values, target):
    buffer = jnp.zeros((EXPERTS * N_EXPERT * CAP, D), values.dtype).at[target].set(values)
    return buffer.reshape(EXPERTS, N_EXPERT * CAP, D)

def layer_forward(inputs, routes, gates, gain, w_gate, w_up, w_down):
    stream = inputs.astype(jnp.float32)
    normed = (stream * norm_scale(stream) * gain).astype(jnp.bfloat16)
    target = slot_index(routes)
    buffer = to_buffer(jnp.repeat(normed, TOP, axis=0), target)
    results = lax.map(lambda pack: expert_forward(*pack), (buffer, w_gate, w_up, w_down))
    picked = results.reshape(-1, D)[target].reshape(TOKENS, TOP, D).astype(jnp.float32)
    return (stream + lax.optimization_barrier(jnp.sum(gates[:, :, None] * picked, axis=1))).astype(jnp.bfloat16)

def layer_backward(inputs, grad, routes, gates, gain, w_gate, w_up, w_down):
    stream = inputs.astype(jnp.float32)
    scale = norm_scale(stream)
    normed = (stream * scale * gain).astype(jnp.bfloat16)
    grad_stream = grad.astype(jnp.float32)
    scaled = (gates[:, :, None] * grad_stream[:, None, :]).astype(jnp.bfloat16).reshape(-1, D)
    target = slot_index(routes)
    row_buffer = to_buffer(jnp.repeat(normed, TOP, axis=0), target)
    grad_buffer = to_buffer(scaled, target)
    results = lax.map(lambda pack: expert_backward(*pack), (row_buffer, grad_buffer, w_gate, w_up, w_down))
    picked = results.reshape(-1, D)[target].reshape(TOKENS, TOP, D).astype(jnp.float32)
    summed = gain * lax.optimization_barrier(jnp.sum(picked, axis=1))
    inner = lax.optimization_barrier(jnp.mean(summed * stream, axis=-1, keepdims=True))
    return (grad_stream + scale * summed - stream * scale * scale * scale * inner).astype(jnp.bfloat16)

def reference(fwd_input, fwd_routes, fwd_gates, bwd_input, bwd_grad, bwd_routes, bwd_gates, norm_gain, w_gate, w_up, w_down):
    outputs = []
    gradients = []
    for layer in range(LAYERS):
        outputs.append(layer_forward(fwd_input[layer], fwd_routes[layer], fwd_gates[layer], norm_gain[layer], w_gate[layer], w_up[layer], w_down[layer]))
        gradients.append(layer_backward(bwd_input[layer], bwd_grad[layer], bwd_routes[layer], bwd_gates[layer], norm_gain[layer], w_gate[layer], w_up[layer], w_down[layer]))
    fwd_out = jnp.roll(jnp.stack(outputs), 1, axis=0)
    bwd_out = jnp.roll(jnp.stack(gradients), -1, axis=0)
    return (fwd_out, bwd_out)
```

```python
import functools

import jax
import jax.numpy as jnp
from jax import lax
from jax.experimental import pallas as pl
from jax.experimental.pallas import tpu as pltpu
from jax.sharding import PartitionSpec as P

EPSILON = 1e-06
BF16 = jnp.bfloat16
F32 = jnp.float32


def inner_size(experts):
    inner = 1
    while inner * inner * 4 <= experts and experts % (inner * 2) == 0:
        inner *= 2
    return inner


def partner(place, step, size, back=False):
    if size & (size - 1) == 0:
        return place ^ step
    return (place + (size - step if back else step)) % size


def over_outer(block, step, outer, inner):
    route = [
        (o * inner + i, partner(o, step, outer) * inner + i)
        for o in range(outer)
        for i in range(inner)
    ]
    return lax.ppermute(block, "expert", route)


def over_inner(block, step, outer, inner, back=False):
    route = [
        (o * inner + i, o * inner + partner(i, step, inner, back))
        for o in range(outer)
        for i in range(inner)
    ]
    return lax.ppermute(block, "expert", route)


def home_and_along(block, step, outer, inner, distance):
    segments = lax.axis_size("segment")
    experts = outer * inner
    route = [
        (
            s * experts + o * inner + i,
            (s + distance) % segments * experts + partner(o, step, outer, True) * inner + i,
        )
        for s in range(segments)
        for o in range(outer)
        for i in range(inner)
    ]
    return lax.ppermute(block, ("segment", "expert"), route)


def along(block, distance):
    segments = lax.axis_size("segment")
    return lax.ppermute(
        block, "segment", [(s, (s + distance) % segments) for s in range(segments)]
    )


def norm_scale(stream):
    return lax.rsqrt(jnp.mean(stream * stream, axis=-1, keepdims=True) + EPSILON)


def dot(left, right):
    return jnp.dot(left, right, preferred_element_type=F32)


def dot_nt(left, right):
    return lax.dot_general(left, right, (((1,), (1,)), ((), ())), preferred_element_type=F32)


def call(kernel, out_shape, args, scratch=(), smem=(), cost=None, limit=32 * 2**20):
    return pl.pallas_call(
        kernel,
        out_shape=out_shape,
        in_specs=[pl.BlockSpec(memory_space=pltpu.VMEM)] * len(args),
        out_specs=jax.tree.map(lambda _: pl.BlockSpec(memory_space=pltpu.VMEM), out_shape),
        scratch_shapes=list(scratch),
        compiler_params=pltpu.CompilerParams(vmem_limit_bytes=limit),
        cost_estimate=cost,
    )(*args)


def shape(*dims, dtype=BF16):
    return jax.ShapeDtypeStruct(dims, dtype)


def prepare_kernel(experts, fr, fg, br, bg, fx, bx, gain, info, fn, bn):
    tokens, width = info.shape
    lane = lax.broadcasted_iota(jnp.int32, (tokens, width), 1)
    gates = jnp.zeros((tokens, width), F32)
    chosen = jnp.zeros((tokens, width), jnp.bool_)
    for base, routes, values in ((0, fr, fg), (2 * experts, br, bg)):
        for k in range(routes.shape[1]):
            route = routes[:, k : k + 1]
            gates = jnp.where(lane == route + base, values[:, k : k + 1], gates)
            chosen = chosen | (lane == route + (base + experts))
    below = lax.broadcasted_iota(jnp.int32, (tokens, tokens), 1) < lax.broadcasted_iota(
        jnp.int32, (tokens, tokens), 0
    )
    rank = dot(below.astype(BF16), chosen.astype(F32).astype(BF16))
    is_slot = (lane // experts) % 2 == 1
    info[...] = jnp.where(is_slot, jnp.where(chosen, rank, -1.0), gates)
    for source, target in ((fx, fn), (bx, bn)):
        stream = source[...].astype(F32)
        target[...] = (stream * norm_scale(stream) * gain[...]).astype(BF16)


def prepare(experts, *args):
    tokens, width = args[4].shape
    lanes = -(-4 * experts // 128) * 128
    row = shape(tokens, width)
    return call(
        functools.partial(prepare_kernel, experts),
        (shape(tokens, lanes, dtype=F32), row, row),
        args,
    )


def my_expert(step, outer, inner):
    me = lax.axis_index("expert")
    o, i = me // inner, me % inner
    return o * inner + partner(i, step, inner)


def select_kernel(outer, inner, capacity, base, gated, *refs):
    infos, rows = refs[:outer], refs[outer : 2 * outer]
    outs, (flat, table) = refs[2 * outer : 2 * outer + inner], refs[2 * outer + inner :]
    experts = outer * inner
    tokens = rows[0].shape[0]
    total = outer * tokens
    for k in range(outer):
        flat[pl.ds(k * tokens, tokens), :] = rows[k][...]
        table[:, pl.ds(k * tokens, tokens)] = infos[k][...].T
    shift = lax.broadcasted_iota(jnp.int32, (1, total), 1) // tokens * capacity
    slots = outer * capacity
    place = lax.broadcasted_iota(jnp.int32, (slots, total), 0)
    for j in range(inner):
        expert = my_expert(j, outer, inner)
        rank = table[pl.ds(base + experts + expert, 1), :].astype(jnp.int32)
        slot = jnp.where(rank >= 0, rank + shift, -1)
        hit = (slot == place).astype(F32)
        picked = dot(hit.astype(BF16), flat[...])
        if gated:
            gate = table[pl.ds(base + expert, 1), :]
            picked = jnp.sum(hit * gate, axis=1, keepdims=True) * picked
        outs[j][...] = picked.astype(BF16)


def select(infos, rows, inner, capacity, base, gated):
    outer = len(rows)
    tokens, width = rows[0].shape
    lanes = infos[0].shape[1]
    return call(
        functools.partial(select_kernel, outer, inner, capacity, base, gated),
        [shape(outer * capacity, width)] * inner,
        (*infos, *rows),
        scratch=(
            pltpu.VMEM((outer * tokens, width), BF16),
            pltpu.VMEM((lanes, outer * tokens), F32),
        ),
    )


def chunks(size, want):
    step = want if size % want == 0 else size
    return [pl.ds(start, step) for start in range(0, size, step)]


def forward_kernel(inner, *refs):
    rows, (w_gate, w_up, w_down) = refs[:inner], refs[inner : inner + 3]
    outs, (flat, hidden) = refs[inner + 3 : 2 * inner + 3], refs[2 * inner + 3 :]
    count = rows[0].shape[0]
    for j in range(inner):
        flat[pl.ds(j * count, count), :] = rows[j][...]
    for part in chunks(w_gate.shape[1], 256):
        gate = dot(flat[...], w_gate[:, part])
        upward = dot(flat[...], w_up[:, part])
        hidden[:, part] = (gate * jax.nn.sigmoid(gate) * upward).astype(BF16)
    for part in chunks(w_down.shape[1], 256):
        result = dot(hidden[...], w_down[:, part]).astype(BF16)
        for j in range(inner):
            outs[j][:, part] = result[j * count : (j + 1) * count]


def expert_forward(rows, w_gate, w_up, w_down):
    inner = len(rows)
    count, width = rows[0].shape
    hidden = w_gate.shape[1]
    return call(
        functools.partial(forward_kernel, inner),
        [shape(count, width)] * inner,
        (*rows, w_gate, w_up, w_down),
        scratch=(
            pltpu.VMEM((inner * count, width), BF16),
            pltpu.VMEM((inner * count, hidden), BF16),
        ),
        cost=pl.CostEstimate(
            flops=6 * inner * count * width * hidden,
            bytes_accessed=6 * width * hidden + 4 * inner * count * width,
            transcendentals=inner * count * hidden,
        ),
    )


def backward_kernel(inner, *refs):
    rows, grads = refs[:inner], refs[inner : 2 * inner]
    w_gate, w_up, w_down = refs[2 * inner : 2 * inner + 3]
    outs, (flat, flat_grad, d_gate, d_up) = refs[2 * inner + 3 : 3 * inner + 3], refs[3 * inner + 3 :]
    count = rows[0].shape[0]
    for j in range(inner):
        flat[pl.ds(j * count, count), :] = rows[j][...]
        flat_grad[pl.ds(j * count, count), :] = grads[j][...]
    for part in chunks(w_gate.shape[1], 256):
        gate = dot(flat[...], w_gate[:, part])
        upward = dot(flat[...], w_up[:, part])
        d_hidden = dot_nt(flat_grad[...], w_down[part, :])
        sigma = jax.nn.sigmoid(gate)
        d_gate[:, part] = (d_hidden * upward * sigma * (1.0 + gate * (1.0 - sigma))).astype(BF16)
        d_up[:, part] = (d_hidden * gate * sigma).astype(BF16)
    for part in chunks(w_gate.shape[0], 256):
        result = dot_nt(d_gate[...], w_gate[part, :]) + dot_nt(d_up[...], w_up[part, :])
        result = result.astype(BF16)
        for j in range(inner):
            outs[j][:, part] = result[j * count : (j + 1) * count]


def expert_backward(rows, grads, w_gate, w_up, w_down):
    inner = len(rows)
    count, width = rows[0].shape
    hidden = w_gate.shape[1]
    return call(
        functools.partial(backward_kernel, inner),
        [shape(count, width)] * inner,
        (*rows, *grads, w_gate, w_up, w_down),
        scratch=[pltpu.VMEM((inner * count, width), BF16)] * 2
        + [pltpu.VMEM((inner * count, hidden), BF16)] * 2,
        cost=pl.CostEstimate(
            flops=10 * inner * count * width * hidden,
            bytes_accessed=6 * width * hidden + 6 * inner * count * width,
            transcendentals=inner * count * hidden,
        ),
    )


def combine_kernel(outer, inner, capacity, base, gated, *refs):
    infos, results = refs[:outer], refs[outer : outer + inner]
    outs, (flat,) = refs[outer + inner : 2 * outer + inner], refs[2 * outer + inner :]
    experts = outer * inner
    tokens, lanes = infos[0].shape
    total = outer * tokens
    slots = outer * capacity
    for k in range(outer):
        flat[pl.ds(k * tokens, tokens), :] = infos[k][...]
    lane = lax.broadcasted_iota(jnp.int32, (total, lanes), 1)
    shift = lax.broadcasted_iota(jnp.int32, (total, 1), 0) // tokens * capacity
    place = lax.broadcasted_iota(jnp.int32, (total, slots), 1)
    summed = None
    for j in range(inner):
        expert = my_expert(j, outer, inner)
        column = jnp.where(lane == base + experts + expert, flat[...], 0.0)
        rank = jnp.sum(column, axis=1, keepdims=True).astype(jnp.int32)
        slot = jnp.where(rank >= 0, rank + shift, -1)
        hit = (slot == place).astype(F32).astype(BF16)
        spread = dot(hit, results[j][...])
        if gated:
            column = jnp.where(lane == base + expert, flat[...], 0.0)
            spread = jnp.sum(column, axis=1, keepdims=True) * spread
        summed = spread if summed is None else summed + spread
    for k in range(outer):
        outs[k][...] = summed[k * tokens : (k + 1) * tokens].astype(BF16)


def combine(infos, results, capacity, base, gated):
    outer, inner = len(infos), len(results)
    tokens, lanes = infos[0].shape
    return call(
        functools.partial(combine_kernel, outer, inner, capacity, base, gated),
        [shape(tokens, results[0].shape[1])] * outer,
        (*infos, *results),
        scratch=(pltpu.VMEM((outer * tokens, lanes), F32),),
    )


def output_kernel(stream, *refs):
    out = refs[-1]
    total = stream[...].astype(F32)
    parts = refs[0][...].astype(F32)
    for part in refs[1:-1]:
        parts = parts + part[...].astype(F32)
    out[0] = (total + parts).astype(BF16)


def gradient_kernel(source, grad, gain, *refs):
    out = refs[-1]
    stream = source[...].astype(F32)
    scale = norm_scale(stream)
    parts = refs[0][...].astype(F32)
    for part in refs[1:-1]:
        parts = parts + part[...].astype(F32)
    summed = gain[...] * parts
    inner = jnp.mean(summed * stream, axis=-1, keepdims=True)
    out[0] = (
        grad[...].astype(F32) + scale * summed - stream * (scale * scale * scale * inner)
    ).astype(BF16)


def on_device(
    fwd_input,
    fwd_routes,
    fwd_gates,
    bwd_input,
    bwd_grad,
    bwd_routes,
    bwd_gates,
    norm_gain,
    w_gate,
    w_up,
    w_down,
):
    experts = lax.axis_size("expert")
    inner = inner_size(experts)
    outer = experts // inner
    tokens, width = fwd_input.shape[1:]
    capacity = min(tokens, tokens * fwd_routes.shape[2] // experts)
    fx, bx, grad = fwd_input[0], bwd_input[0], bwd_grad[0]
    weights = (w_gate[0, 0], w_up[0, 0], w_down[0, 0])

    def gathered(block):
        return [block] + [over_outer(block, k, outer, inner) for k in range(1, outer)]

    def exchanged(blocks, back=False):
        return [blocks[0]] + [
            over_inner(blocks[j], j, outer, inner, back) for j in range(1, inner)
        ]

    def returned(blocks, distance):
        return [
            home_and_along(blocks[k], k, outer, inner, distance) for k in range(outer)
        ]

    all_grad = gathered(grad)
    info, f_normed, b_normed = prepare(
        experts, fwd_routes[0], fwd_gates[0], bwd_routes[0], bwd_gates[0], fx, bx, norm_gain
    )
    infos = gathered(info)
    all_b = gathered(b_normed)
    all_f = gathered(f_normed)
    fx_next = along(fx, 1)
    bx_next, grad_next, gain_next = along(bx, -1), along(grad, -1), along(norm_gain, -1)

    b_base = 2 * experts
    grads = exchanged(select(infos, all_grad, inner, capacity, b_base, True))
    b_rows = exchanged(select(infos, all_b, inner, capacity, b_base, False))
    f_rows = exchanged(select(infos, all_f, inner, capacity, 0, False))
    b_back = exchanged(expert_backward(b_rows, grads, *weights), True)
    f_back = exchanged(expert_forward(f_rows, *weights), True)
    b_parts = returned(combine(infos, b_back, capacity, b_base, False), -1)
    f_parts = returned(combine(infos, f_back, capacity, 0, True), 1)
    out = shape(1, tokens, width)
    backward_next = call(gradient_kernel, out, (bx_next, grad_next, gain_next, *b_parts))
    forward_next = call(output_kernel, out, (fx_next, *f_parts))
    return (forward_next, backward_next)


def solution(mesh):
    placed = (
        P("segment", "expert", None),
        P("segment", "expert", None),
        P("segment", "expert", None),
        P("segment", "expert", None),
        P("segment", "expert", None),
        P("segment", "expert", None),
        P("segment", "expert", None),
        P("segment", None),
        P("segment", "expert", None, None),
        P("segment", "expert", None, None),
        P("segment", "expert", None, None),
    )
    return jax.shard_map(
        on_device,
        mesh=mesh,
        in_specs=placed,
        out_specs=(P("segment", "expert", None), P("segment", "expert", None)),
        check_vma=False,
    )
```

```python
import functools

import jax
import jax.numpy as jnp
from jax import lax
from jax.experimental import pallas as pl
from jax.experimental.pallas import tpu as pltpu
from jax.sharding import PartitionSpec as P

EPSILON = 1e-06
BF16 = jnp.bfloat16
F32 = jnp.float32


def inner_size(experts):
    inner = 1
    while inner * inner * 4 <= experts and experts % (inner * 2) == 0:
        inner *= 2
    return inner


def partner(place, step, size, back=False):
    if size & (size - 1) == 0:
        return place ^ step
    return (place + (size - step if back else step)) % size


def over_outer(block, step, outer, inner):
    route = [
        (o * inner + i, partner(o, step, outer) * inner + i)
        for o in range(outer)
        for i in range(inner)
    ]
    return lax.ppermute(block, "expert", route)


def over_inner(block, step, outer, inner, back=False):
    route = [
        (o * inner + i, o * inner + partner(i, step, inner, back))
        for o in range(outer)
        for i in range(inner)
    ]
    return lax.ppermute(block, "expert", route)


def home_and_along(block, step, outer, inner, distance):
    segments = lax.axis_size("segment")
    experts = outer * inner
    route = [
        (
            s * experts + o * inner + i,
            (s + distance) % segments * experts + partner(o, step, outer, True) * inner + i,
        )
        for s in range(segments)
        for o in range(outer)
        for i in range(inner)
    ]
    return lax.ppermute(block, ("segment", "expert"), route)


def after(values, *others):
    return lax.optimization_barrier((values, others))[0]


def norm_scale(stream):
    return lax.rsqrt(jnp.mean(stream * stream, axis=-1, keepdims=True) + EPSILON)


def dot(left, right):
    return jnp.dot(left, right, preferred_element_type=F32)


def dot_nt(left, right):
    return lax.dot_general(left, right, (((1,), (1,)), ((), ())), preferred_element_type=F32)


def call(kernel, out_shape, args, far=(), scratch=(), cost=None, limit=16 * 2**20):
    near = pl.BlockSpec(memory_space=pltpu.VMEM)
    return pl.pallas_call(
        kernel,
        out_shape=out_shape,
        in_specs=[near] * len(args) + [pl.BlockSpec(memory_space=pltpu.HBM)] * len(far),
        out_specs=jax.tree.map(lambda _: near, out_shape),
        scratch_shapes=[
            *scratch,
            *(pltpu.VMEM(v.shape, v.dtype) for v in far),
            *([pltpu.SemaphoreType.DMA((len(far),))] if far else []),
        ],
        compiler_params=pltpu.CompilerParams(vmem_limit_bytes=limit),
        cost_estimate=cost or pl.CostEstimate(flops=2**31, bytes_accessed=2**22, transcendentals=0),
    )(*args, *far)


def fetches(sources, targets, semaphores):
    copies = [
        pltpu.make_async_copy(source, target, semaphores.at[i])
        for i, (source, target) in enumerate(zip(sources, targets))
    ]
    for copy in copies:
        copy.start()
    return copies


def shape(*dims, dtype=BF16):
    return jax.ShapeDtypeStruct(dims, dtype)


def my_expert(step, outer, inner):
    me = lax.axis_index("expert")
    o, i = me // inner, me % inner
    return o * inner + partner(i, step, inner)


def normed_rows(rows, gain):
    stream = rows.astype(F32)
    return (stream * norm_scale(stream) * gain).astype(BF16)


def fill_table(experts, table, lists):
    tokens = table.shape[1]
    row = lax.broadcasted_iota(jnp.int32, (experts, tokens), 0)
    before = lax.broadcasted_iota(jnp.int32, (tokens, tokens), 0) < lax.broadcasted_iota(
        jnp.int32, (tokens, tokens), 1
    )
    before = before.astype(F32).astype(BF16)
    for side, (routes, values) in enumerate((lists[:2], lists[2:])):
        rest = jnp.zeros((experts, tokens), F32)
        chosen = jnp.zeros((experts, tokens), jnp.bool_)
        for k in range(routes.shape[0]):
            here = row == routes[k : k + 1, :]
            rest = jnp.where(here, values[k : k + 1, :], rest)
            chosen = chosen | here
        base = 4 * experts * side
        for term in range(3):
            rounded = rest.astype(BF16).astype(F32)
            table[pl.ds(base + term * experts, experts), :] = rounded
            rest = rest - rounded
        rank = dot(chosen.astype(F32).astype(BF16), before)
        table[pl.ds(base + 3 * experts, experts), :] = jnp.where(chosen, rank, -1.0)


def picked(table, side, expert, experts, blocks, capacity):
    total = table.shape[1]
    shift = lax.broadcasted_iota(jnp.int32, (1, total), 1) // (total // blocks) * capacity
    place = lax.broadcasted_iota(jnp.int32, (blocks * capacity, total), 0)
    rank = table[pl.ds((4 * side + 3) * experts + expert, 1), :].astype(jnp.int32)
    return (jnp.where(rank >= 0, rank + shift, -1) == place).astype(F32)


def gate_of(table, side, expert, experts):
    terms = [table[pl.ds((4 * side + term) * experts + expert, 1), :] for term in range(3)]
    return terms[0] + terms[1] + terms[2]


def prepare_kernel(outer, inner, capacity, *refs):
    far, (f_pack, b_pack, home), own = refs[:8], refs[8:11], refs[11 : 11 + inner]
    table, *near, semaphores = refs[11 + inner :]
    experts = outer * inner
    copies = fetches(far, near, semaphores)
    lists, (fx, bx, grad, gain) = near[:4], near[4:]
    tokens, width = fx.shape
    for copy in copies:
        copy.wait()
    fill_table(experts, table, lists)
    f_pack[:, pl.ds(width, table.shape[0])] = table[...].T.astype(BF16)
    f_pack[:, pl.ds(0, width)] = normed_rows(fx[...], gain[...])
    b_pack[pl.ds(0, tokens), :] = normed_rows(bx[...], gain[...])
    b_pack[pl.ds(tokens, tokens), :] = grad[...]
    home[pl.ds(0, tokens), :] = bx[...]
    home[pl.ds(tokens, tokens), :] = grad[...]
    for j in range(inner):
        expert = my_expert(j, outer, inner)
        f_hit = picked(table, 0, expert, experts, 1, capacity).astype(BF16)
        b_hit = picked(table, 1, expert, experts, 1, capacity)
        gate = jnp.sum(b_hit * gate_of(table, 1, expert, experts), axis=1, keepdims=True)
        b_hit = b_hit.astype(BF16)
        own[j][pl.ds(0, capacity), :] = dot(f_hit, f_pack[:, pl.ds(0, width)]).astype(BF16)
        own[j][pl.ds(capacity, capacity), :] = dot(b_hit, b_pack[pl.ds(0, tokens), :]).astype(BF16)
        own[j][pl.ds(2 * capacity, capacity), :] = (gate * dot(b_hit, grad[...])).astype(BF16)


def prepare(outer, inner, capacity, *args):
    tokens, width = args[4].shape
    lanes = 8 * outer * inner
    return call(
        functools.partial(prepare_kernel, outer, inner, capacity),
        [shape(tokens, width + lanes), shape(2 * tokens, width), shape(2 * tokens, width)]
        + [shape(3 * capacity, width)] * inner,
        (),
        args,
        scratch=(pltpu.VMEM((lanes, tokens), F32),),
        limit=60 * 2**20,
    )


def select_kernel(outer, inner, capacity, side, blocks, *refs):
    experts = outer * inner
    packs, rows = refs[:blocks], refs[blocks : 2 * blocks]
    outs, (flat, table) = refs[2 * blocks : 2 * blocks + inner], refs[2 * blocks + inner :]
    tokens, width = packs[0].shape[0], flat.shape[1]
    total = blocks * tokens
    for k in range(blocks):
        table[:, pl.ds(k * tokens, tokens)] = packs[k][:, pl.ds(width, 8 * experts)].astype(F32).T
        for part in range(side + 1):
            flat[pl.ds(part * total + k * tokens, tokens), :] = rows[k][
                pl.ds(part * tokens, tokens), pl.ds(0, width)
            ]
    slots = blocks * capacity
    for j in range(inner):
        expert = my_expert(j, outer, inner)
        hit = picked(table, side, expert, experts, blocks, capacity)
        outs[j][pl.ds(0, slots), :] = dot(hit.astype(BF16), flat[pl.ds(0, total), :]).astype(BF16)
        if side == 1:
            gate = jnp.sum(hit * gate_of(table, 1, expert, experts), axis=1, keepdims=True)
            grads = dot(hit.astype(BF16), flat[pl.ds(total, total), :])
            outs[j][pl.ds(slots, slots), :] = (gate * grads).astype(BF16)


def select(packs, rows, width, outer, inner, capacity, side):
    blocks = len(rows)
    tokens = packs[0].shape[0]
    return call(
        functools.partial(select_kernel, outer, inner, capacity, side, blocks),
        [shape(blocks * capacity * (side + 1), width)] * inner,
        (*packs, *rows),
        scratch=(
            pltpu.VMEM((blocks * tokens * (side + 1), width), BF16),
            pltpu.VMEM((8 * outer * inner, blocks * tokens), F32),
        ),
    )


def chunks(size, want):
    step = want if size % want == 0 else size
    return [pl.ds(start, step) for start in range(0, size, step)]


def load_rows(flat, own, others, groups, capacity, part, parts):
    rest = others[0].shape[0] // parts
    first = 0 if parts == 1 else part + 1
    at = 0
    for j, k in [(j, k) for group in groups for j in range(len(own)) for k in group]:
        if k == 0:
            rows = own[j][pl.ds(first * capacity, capacity), :]
        else:
            rows = others[j][pl.ds(part * rest + (k - 1) * capacity, capacity), :]
        flat[pl.ds(at, capacity), :] = rows
        at += capacity


def forward_kernel(inner, blocks, capacity, *refs):
    own, others, (w_gate, w_up, w_down) = (
        refs[:inner],
        refs[inner : 2 * inner],
        refs[2 * inner : 2 * inner + 3],
    )
    outs, (flat, hidden) = refs[2 * inner + 3 : 3 * inner + 3], refs[3 * inner + 3 :]
    load_rows(flat, own, others, (blocks,), capacity, 0, 1)
    for part in chunks(w_gate.shape[1], 256):
        gate = dot(flat[...], w_gate[:, part])
        upward = dot(flat[...], w_up[:, part])
        hidden[:, part] = (gate * jax.nn.sigmoid(gate) * upward).astype(BF16)
    count = outs[0].shape[0]
    for part in chunks(w_down.shape[1], 256):
        result = dot(hidden[...], w_down[:, part]).astype(BF16)
        for j in range(inner):
            outs[j][:, part] = result[j * count : (j + 1) * count]


def expert_forward(own, others, weights, blocks, capacity):
    inner = len(own)
    count = len(blocks) * capacity
    width, hidden = weights[0].shape
    return call(
        functools.partial(forward_kernel, inner, blocks, capacity),
        [shape(count, width)] * inner,
        (*own, *others, *weights),
        scratch=(
            pltpu.VMEM((inner * count, width), BF16),
            pltpu.VMEM((inner * count, hidden), BF16),
        ),
        cost=pl.CostEstimate(
            flops=6 * inner * count * width * hidden,
            bytes_accessed=6 * width * hidden + 4 * inner * count * width,
            transcendentals=inner * count * hidden,
        ),
    )


def backward_kernel(inner, groups, capacity, *refs):
    own, others, (w_gate, w_up, w_down) = (
        refs[:inner],
        refs[inner : 2 * inner],
        refs[2 * inner : 2 * inner + 3],
    )
    outs, (flat, flat_grad, d_gate, d_up) = refs[2 * inner + 3 : -4], refs[-4:]
    load_rows(flat, own, others, groups, capacity, 0, 2)
    load_rows(flat_grad, own, others, groups, capacity, 1, 2)
    for part in chunks(w_gate.shape[1], 256):
        gate = dot(flat[...], w_gate[:, part])
        upward = dot(flat[...], w_up[:, part])
        d_hidden = dot_nt(flat_grad[...], w_down[part, :])
        sigma = jax.nn.sigmoid(gate)
        d_gate[:, part] = (d_hidden * upward * sigma * (1.0 + gate * (1.0 - sigma))).astype(BF16)
        d_up[:, part] = (d_hidden * gate * sigma).astype(BF16)
    for part in chunks(w_gate.shape[0], 256):
        result = dot_nt(d_gate[...], w_gate[part, :]) + dot_nt(d_up[...], w_up[part, :])
        result = result.astype(BF16)
        at = 0
        for out in outs:
            out[:, part] = result[at : at + out.shape[0]]
            at += out.shape[0]


def expert_backward(own, others, weights, groups, capacity):
    inner = len(own)
    count = sum(len(group) for group in groups) * capacity
    width, hidden = weights[0].shape
    outs = call(
        functools.partial(backward_kernel, inner, groups, capacity),
        [shape(len(group) * capacity, width) for group in groups for _ in range(inner)],
        (*own, *others, *weights),
        scratch=[pltpu.VMEM((inner * count, width), BF16)] * 2
        + [pltpu.VMEM((inner * count, hidden), BF16)] * 2,
        cost=pl.CostEstimate(
            flops=10 * inner * count * width * hidden,
            bytes_accessed=6 * width * hidden + 6 * inner * count * width,
            transcendentals=inner * count * hidden,
        ),
    )
    return outs[:inner], outs[inner:]


def combine_kernel(blocks, experts, inner, capacity, side, *refs):
    packs, results = refs[:blocks], refs[blocks : blocks + inner]
    gain, home = refs[blocks + inner : blocks + inner + 2]
    outs, flat = refs[blocks + inner + 2 : -1], refs[-1]
    tokens, lanes = packs[0].shape[0], flat.shape[1]
    width = packs[0].shape[1] - lanes
    total = blocks * tokens
    slots = blocks * capacity
    for k in range(blocks):
        flat[pl.ds(k * tokens, tokens), :] = packs[k][:, pl.ds(width, lanes)].astype(F32)
    lane = lax.broadcasted_iota(jnp.int32, (total, lanes), 1)
    shift = lax.broadcasted_iota(jnp.int32, (total, 1), 0) // tokens * capacity
    place = lax.broadcasted_iota(jnp.int32, (total, slots), 1)
    summed = None
    for j in range(inner):
        first = 4 * experts * side + my_expert(j, experts // inner, inner)
        column = jnp.where(lane == first + 3 * experts, flat[...], 0.0)
        rank = jnp.sum(column, axis=1, keepdims=True).astype(jnp.int32)
        slot = jnp.where(rank >= 0, rank + shift, -1)
        hit = (slot == place).astype(F32).astype(BF16)
        spread = dot(hit, results[j][...])
        if side == 0:
            terms = (lane == first) | (lane == first + experts) | (lane == first + 2 * experts)
            column = jnp.where(terms, flat[...], 0.0)
            spread = jnp.sum(column, axis=1, keepdims=True) * spread
        summed = spread if summed is None else summed + spread
    if side == 1:
        summed = gain[...] * summed
    for k in range(blocks):
        part = summed[k * tokens : (k + 1) * tokens]
        if outs[k].dtype == F32:
            outs[k][...] = home[...].astype(F32) + part
        else:
            outs[k][pl.ds(0, tokens), :] = part.astype(BF16)
            if outs[k].shape[0] > tokens:
                outs[k][pl.ds(tokens, 2 * tokens), :] = home[...]


def combine(packs, results, gain, home, steps, inner, capacity, side):
    packs = [packs[k] for k in steps]
    blocks = len(packs)
    tokens, width = packs[0].shape[0], results[0].shape[1]
    lanes = packs[0].shape[1] - width
    local = shape(3 * tokens, width) if side == 1 else shape(tokens, width, dtype=F32)
    return call(
        functools.partial(combine_kernel, blocks, lanes // 8, inner, capacity, side),
        [shape(tokens, width) if k else local for k in steps],
        (*packs, *results, gain, home),
        scratch=(pltpu.VMEM((blocks * tokens, lanes), F32),),
    )


def output_kernel(*refs):
    total = refs[-2][...]
    for part in refs[:-2]:
        total = total + part[...].astype(F32)
    refs[-1][0] = total.astype(BF16)


def gradient_kernel(*refs):
    local, out = refs[-2:]
    tokens = out.shape[1]
    summed, stream, grad = (
        local[pl.ds(i * tokens, tokens), :].astype(F32) for i in range(3)
    )
    scale = norm_scale(stream)
    for part in refs[:-2]:
        summed = summed + part[...].astype(F32)
    inner = jnp.mean(summed * stream, axis=-1, keepdims=True)
    out[0] = (grad + scale * summed - stream * (scale * scale * scale * inner)).astype(BF16)


def on_device(
    fwd_input,
    fwd_routes,
    fwd_gates,
    bwd_input,
    bwd_grad,
    bwd_routes,
    bwd_gates,
    norm_gain,
    w_gate,
    w_up,
    w_down,
):
    experts = lax.axis_size("expert")
    inner = inner_size(experts)
    outer = experts // inner
    tokens, width = fwd_input.shape[1:]
    capacity = min(tokens, tokens * fwd_routes.shape[2] // experts)
    fx, bx, grad = fwd_input[0], bwd_input[0], bwd_grad[0]
    weights = (w_gate[0, 0], w_up[0, 0], w_down[0, 0])

    def spread(block):
        return [over_outer(block, k, outer, inner) for k in range(1, outer)]

    def exchanged(blocks, back=False):
        return [blocks[0]] + [
            over_inner(blocks[j], j, outer, inner, back) for j in range(1, inner)
        ]

    def returned(blocks, steps, distance):
        return [
            home_and_along(block, k, outer, inner, distance) for k, block in zip(steps, blocks)
        ]

    lists = [v[0].T for v in (fwd_routes, fwd_gates, bwd_routes, bwd_gates)]
    f_pack, b_pack, home, *own = prepare(
        outer, inner, capacity, *lists, fx, bx, grad, norm_gain
    )
    f_away = spread(f_pack)
    own = exchanged(own)
    b_away = spread(after(b_pack, f_away[0]))

    sizes = (width, outer, inner, capacity)
    f_rows = exchanged(select(f_away, f_away, *sizes, 0))
    every = (*range(1, outer), 0)
    f_back = exchanged(expert_forward(own, f_rows, weights, every, capacity), True)
    b_away, f_back = after((b_away, f_back))
    b_picked = select(f_away, b_away, *sizes, 1)
    b_rows = exchanged(b_picked)
    packs = [f_pack] + f_away
    f_sums = combine(packs, after(f_back, b_picked[0]), norm_gain, fx, every, inner, capacity, 0)
    f_parts = returned(f_sums, every, 1)
    b_rows = after(b_rows, f_parts)
    half = outer // 2
    groups = ((half,), (*range(1, half), *range(half + 1, outer), 0))
    first, last = expert_backward(own, b_rows, weights, groups, capacity)
    b_back = exchanged(first, True)
    out = shape(1, tokens, width)
    forward_next = call(output_kernel, out, f_parts)
    b_back = after(b_back, forward_next)
    b_sums = combine(packs, b_back, norm_gain, home, groups[0], inner, capacity, 1)
    b_parts = returned(b_sums, groups[0], -1)
    b_last = after(exchanged(after(last, b_sums[0]), True), b_parts[0])
    b_sums = combine(packs, b_last, norm_gain, home, groups[1], inner, capacity, 1)
    b_parts += returned(b_sums, groups[1], -1)
    backward_next = call(gradient_kernel, out, b_parts)
    return (forward_next, backward_next)


def solution(mesh):
    placed = (
        P("segment", "expert", None),
        P("segment", "expert", None),
        P("segment", "expert", None),
        P("segment", "expert", None),
        P("segment", "expert", None),
        P("segment", "expert", None),
        P("segment", "expert", None),
        P("segment", None),
        P("segment", "expert", None, None),
        P("segment", "expert", None, None),
        P("segment", "expert", None, None),
    )
    return jax.shard_map(
        on_device,
        mesh=mesh,
        in_specs=placed,
        out_specs=(P("segment", "expert", None), P("segment", "expert", None)),
        check_vma=False,
    )
```

```python
import functools

import jax
import jax.numpy as jnp
from jax import lax
from jax.experimental import pallas as pl
from jax.experimental.pallas import tpu as pltpu
from jax.sharding import PartitionSpec as P

EPSILON = 1e-06
COST = {
    "prepare": 2,
    "local": 2,
    "select": 2,
    "f_expert": 2.25,
    "b_expert": 0.5,
    "combine": 2,
    "output": 2,
    "gradient": 2,
}
BF16 = jnp.bfloat16
F32 = jnp.float32


def inner_size(experts):
    inner = 1
    while inner * inner * 4 <= experts and experts % (inner * 2) == 0:
        inner *= 2
    return inner


def partner(place, step, size, back=False):
    if size & (size - 1) == 0:
        return place ^ step
    return (place + (size - step if back else step)) % size


def over_outer(block, step, outer, inner):
    route = [
        (o * inner + i, partner(o, step, outer) * inner + i)
        for o in range(outer)
        for i in range(inner)
    ]
    return lax.ppermute(block, "expert", route)


def over_inner(block, step, outer, inner, back=False):
    route = [
        (o * inner + i, o * inner + partner(i, step, inner, back))
        for o in range(outer)
        for i in range(inner)
    ]
    return lax.ppermute(block, "expert", route)


def home_and_along(block, step, outer, inner, distance):
    segments = lax.axis_size("segment")
    experts = outer * inner
    route = [
        (
            s * experts + o * inner + i,
            (s + distance) % segments * experts + partner(o, step, outer, True) * inner + i,
        )
        for s in range(segments)
        for o in range(outer)
        for i in range(inner)
    ]
    return lax.ppermute(block, ("segment", "expert"), route)


def after(values, *others):
    return lax.optimization_barrier((values, others))[0]


def norm_scale(stream):
    return lax.rsqrt(jnp.mean(stream * stream, axis=-1, keepdims=True) + EPSILON)


def dot(left, right):
    return jnp.dot(left, right, preferred_element_type=F32)


def dot_nt(left, right):
    return lax.dot_general(left, right, (((1,), (1,)), ((), ())), preferred_element_type=F32)


def call(kernel, out_shape, args, cost, far=(), scratch=(), limit=16 * 2**20):
    near = pl.BlockSpec(memory_space=pltpu.VMEM)
    return pl.pallas_call(
        kernel,
        out_shape=out_shape,
        in_specs=[near] * len(args) + [pl.BlockSpec(memory_space=pltpu.HBM)] * len(far),
        out_specs=jax.tree.map(lambda _: near, out_shape),
        scratch_shapes=[
            *scratch,
            *(pltpu.VMEM(v.shape, v.dtype) for v in far),
            *([pltpu.SemaphoreType.DMA((len(far),))] if far else []),
        ],
        compiler_params=pltpu.CompilerParams(vmem_limit_bytes=limit),
        cost_estimate=pl.CostEstimate(
            flops=int(cost * 2**30), bytes_accessed=2**16, transcendentals=0
        ),
    )(*args, *far)


def fetches(sources, targets, semaphores):
    copies = [
        pltpu.make_async_copy(source, target, semaphores.at[i])
        for i, (source, target) in enumerate(zip(sources, targets))
    ]
    for copy in copies:
        copy.start()
    return copies


def shape(*dims, dtype=BF16):
    return jax.ShapeDtypeStruct(dims, dtype)


def my_expert(step, outer, inner):
    me = lax.axis_index("expert")
    o, i = me // inner, me % inner
    return o * inner + partner(i, step, inner)


def normed_rows(rows, gain):
    stream = rows.astype(F32)
    return (stream * norm_scale(stream) * gain).astype(BF16)


def fill_table(experts, table, lists):
    tokens = table.shape[1]
    row = lax.broadcasted_iota(jnp.int32, (experts, tokens), 0)
    before = lax.broadcasted_iota(jnp.int32, (tokens, tokens), 0) < lax.broadcasted_iota(
        jnp.int32, (tokens, tokens), 1
    )
    before = before.astype(F32).astype(BF16)
    for side, (routes, values) in enumerate((lists[:2], lists[2:])):
        rest = jnp.zeros((experts, tokens), F32)
        chosen = jnp.zeros((experts, tokens), jnp.bool_)
        for k in range(routes.shape[0]):
            here = row == routes[k : k + 1, :]
            rest = jnp.where(here, values[k : k + 1, :], rest)
            chosen = chosen | here
        base = 4 * experts * side
        for term in range(3):
            rounded = rest.astype(BF16).astype(F32)
            table[pl.ds(base + term * experts, experts), :] = rounded
            rest = rest - rounded
        rank = dot(chosen.astype(F32).astype(BF16), before)
        table[pl.ds(base + 3 * experts, experts), :] = jnp.where(chosen, rank, -1.0)


def picked(table, side, expert, experts, blocks, capacity):
    total = table.shape[1]
    shift = lax.broadcasted_iota(jnp.int32, (1, total), 1) // (total // blocks) * capacity
    place = lax.broadcasted_iota(jnp.int32, (blocks * capacity, total), 0)
    rank = table[pl.ds((4 * side + 3) * experts + expert, 1), :].astype(jnp.int32)
    return (jnp.where(rank >= 0, rank + shift, -1) == place).astype(F32)


def gate_of(table, side, expert, experts):
    terms = [table[pl.ds((4 * side + term) * experts + expert, 1), :] for term in range(3)]
    return terms[0] + terms[1] + terms[2]


def prepare_kernel(experts, *refs):
    far, (f_pack,) = refs[:6], refs[6:7]
    table, *near, semaphores = refs[7:]
    copies = fetches(far, near, semaphores)
    lists, (fx, gain) = near[:4], near[4:]
    width = fx.shape[1]
    for copy in copies:
        copy.wait()
    f_pack[:, pl.ds(0, width)] = normed_rows(fx[...], gain[...])
    fill_table(experts, table, lists)
    f_pack[:, pl.ds(width, table.shape[0])] = table[...].T.astype(BF16)


def prepare(experts, *args):
    tokens, width = args[4].shape
    lanes = 8 * experts
    return call(
        functools.partial(prepare_kernel, experts),
        [shape(tokens, width + lanes)],
        (),
        COST["prepare"],
        args,
        scratch=(pltpu.VMEM((lanes, tokens), F32),),
        limit=60 * 2**20,
    )[0]


def local_kernel(outer, inner, capacity, *refs):
    f_pack, far = refs[0], refs[1:4]
    (b_pack, home), own = refs[4:6], refs[6 : 6 + inner]
    table, *near, semaphores = refs[6 + inner :]
    experts = outer * inner
    copies = fetches(far, near, semaphores)
    bx, grad, gain = near
    tokens, width = bx.shape
    table[...] = f_pack[:, pl.ds(width, table.shape[0])].astype(F32).T
    for copy in copies:
        copy.wait()
    b_pack[pl.ds(0, tokens), :] = normed_rows(bx[...], gain[...])
    b_pack[pl.ds(tokens, tokens), :] = grad[...]
    home[pl.ds(0, tokens), :] = bx[...]
    home[pl.ds(tokens, tokens), :] = grad[...]
    for j in range(inner):
        expert = my_expert(j, outer, inner)
        f_hit = picked(table, 0, expert, experts, 1, capacity).astype(BF16)
        b_hit = picked(table, 1, expert, experts, 1, capacity)
        gate = jnp.sum(b_hit * gate_of(table, 1, expert, experts), axis=1, keepdims=True)
        b_hit = b_hit.astype(BF16)
        own[j][pl.ds(0, capacity), :] = dot(f_hit, f_pack[:, pl.ds(0, width)]).astype(BF16)
        own[j][pl.ds(capacity, capacity), :] = dot(b_hit, b_pack[pl.ds(0, tokens), :]).astype(BF16)
        own[j][pl.ds(2 * capacity, capacity), :] = (gate * dot(b_hit, grad[...])).astype(BF16)


def local(f_pack, outer, inner, capacity, *args):
    tokens, width = args[0].shape
    lanes = f_pack.shape[1] - width
    return call(
        functools.partial(local_kernel, outer, inner, capacity),
        [shape(2 * tokens, width), shape(2 * tokens, width)]
        + [shape(3 * capacity, width)] * inner,
        (f_pack,),
        COST["local"],
        args,
        scratch=(pltpu.VMEM((lanes, tokens), F32),),
        limit=60 * 2**20,
    )


def select_kernel(outer, inner, capacity, side, blocks, *refs):
    experts = outer * inner
    packs, rows = refs[:blocks], refs[blocks : 2 * blocks]
    outs, (flat, table) = refs[2 * blocks : 2 * blocks + inner], refs[2 * blocks + inner :]
    tokens, width = packs[0].shape[0], flat.shape[1]
    total = blocks * tokens
    for k in range(blocks):
        table[:, pl.ds(k * tokens, tokens)] = packs[k][:, pl.ds(width, 8 * experts)].astype(F32).T
        for part in range(side + 1):
            flat[pl.ds(part * total + k * tokens, tokens), :] = rows[k][
                pl.ds(part * tokens, tokens), pl.ds(0, width)
            ]
    slots = blocks * capacity
    for j in range(inner):
        expert = my_expert(j, outer, inner)
        hit = picked(table, side, expert, experts, blocks, capacity)
        outs[j][pl.ds(0, slots), :] = dot(hit.astype(BF16), flat[pl.ds(0, total), :]).astype(BF16)
        if side == 1:
            gate = jnp.sum(hit * gate_of(table, 1, expert, experts), axis=1, keepdims=True)
            grads = dot(hit.astype(BF16), flat[pl.ds(total, total), :])
            outs[j][pl.ds(slots, slots), :] = (gate * grads).astype(BF16)


def select(packs, rows, width, outer, inner, capacity, side):
    blocks = len(rows)
    tokens = packs[0].shape[0]
    return call(
        functools.partial(select_kernel, outer, inner, capacity, side, blocks),
        [shape(blocks * capacity * (side + 1), width)] * inner,
        (*packs, *rows),
        COST["select"],
        scratch=(
            pltpu.VMEM((blocks * tokens * (side + 1), width), BF16),
            pltpu.VMEM((8 * outer * inner, blocks * tokens), F32),
        ),
    )


def chunks(size, want):
    step = want if size % want == 0 else size
    return [pl.ds(start, step) for start in range(0, size, step)]


def places(inner, groups):
    return [(j, k) for group in groups for j in range(inner) for k in group]


def load_rows(flat, own, others, inner, groups, steps, capacity, part, parts):
    rest = others[0].shape[0] // parts
    first = 0 if parts == 1 else part + 1
    for at, (j, k) in enumerate(places(inner, groups)):
        if k == 0:
            rows = own[j][pl.ds(first * capacity, capacity), :]
        else:
            rows = others[j][pl.ds(part * rest + steps.index(k) * capacity, capacity), :]
        flat[pl.ds(at * capacity, capacity), :] = rows


def store_rows(outs, result, part):
    at = 0
    for out in outs:
        out[:, part] = result[at : at + out.shape[0]]
        at += out.shape[0]


def forward_kernel(inner, groups, steps, capacity, *refs):
    own, others = refs[:inner], refs[inner : 2 * inner]
    w_gate, w_up, w_down = refs[2 * inner : 2 * inner + 3]
    outs, (flat, hidden) = refs[2 * inner + 3 : -2], refs[-2:]
    load_rows(flat, own, others, inner, groups, steps, capacity, 0, 1)
    for part in chunks(w_gate.shape[1], 256):
        gate = dot(flat[...], w_gate[:, part])
        upward = dot(flat[...], w_up[:, part])
        hidden[:, part] = (gate * jax.nn.sigmoid(gate) * upward).astype(BF16)
    for part in chunks(w_down.shape[1], 256):
        store_rows(outs, dot(hidden[...], w_down[:, part]).astype(BF16), part)


def backward_kernel(inner, groups, steps, capacity, *refs):
    own, others = refs[:inner], refs[inner : 2 * inner]
    w_gate, w_up, w_down = refs[2 * inner : 2 * inner + 3]
    outs, (flat, flat_grad, d_gate, d_up) = refs[2 * inner + 3 : -4], refs[-4:]
    load_rows(flat, own, others, inner, groups, steps, capacity, 0, 2)
    load_rows(flat_grad, own, others, inner, groups, steps, capacity, 1, 2)
    for part in chunks(w_gate.shape[1], 256):
        gate = dot(flat[...], w_gate[:, part])
        upward = dot(flat[...], w_up[:, part])
        d_hidden = dot_nt(flat_grad[...], w_down[part, :])
        sigma = jax.nn.sigmoid(gate)
        d_gate[:, part] = (d_hidden * upward * sigma * (1.0 + gate * (1.0 - sigma))).astype(BF16)
        d_up[:, part] = (d_hidden * gate * sigma).astype(BF16)
    for part in chunks(w_gate.shape[0], 256):
        result = dot_nt(d_gate[...], w_gate[part, :]) + dot_nt(d_up[...], w_up[part, :])
        store_rows(outs, result.astype(BF16), part)


def expert(kernel, own, others, weights, groups, steps, capacity, inputs, products, cost):
    inner = len(own)
    count = len(places(inner, groups)) * capacity
    width, hidden = weights[0].shape
    outs = call(
        functools.partial(kernel, inner, groups, steps, capacity),
        [shape(len(group) * capacity, width) for group in groups for _ in range(inner)],
        (*own, *others, *weights),
        scratch=[pltpu.VMEM((count, width), BF16)] * inputs
        + [pltpu.VMEM((count, hidden), BF16)] * inputs,
        cost=cost,
    )
    return [outs[i * inner : (i + 1) * inner] for i in range(len(groups))]


def combine_kernel(blocks, experts, inner, capacity, side, *refs):
    packs, results = refs[:blocks], refs[blocks : blocks + inner]
    gain, home = refs[blocks + inner : blocks + inner + 2]
    outs, flat = refs[blocks + inner + 2 : -1], refs[-1]
    tokens, lanes = packs[0].shape[0], flat.shape[1]
    width = packs[0].shape[1] - lanes
    total = blocks * tokens
    slots = blocks * capacity
    for k in range(blocks):
        flat[pl.ds(k * tokens, tokens), :] = packs[k][:, pl.ds(width, lanes)].astype(F32)
    lane = lax.broadcasted_iota(jnp.int32, (total, lanes), 1)
    shift = lax.broadcasted_iota(jnp.int32, (total, 1), 0) // tokens * capacity
    place = lax.broadcasted_iota(jnp.int32, (total, slots), 1)
    summed = None
    for j in range(inner):
        first = 4 * experts * side + my_expert(j, experts // inner, inner)
        column = jnp.where(lane == first + 3 * experts, flat[...], 0.0)
        rank = jnp.sum(column, axis=1, keepdims=True).astype(jnp.int32)
        slot = jnp.where(rank >= 0, rank + shift, -1)
        hit = (slot == place).astype(F32).astype(BF16)
        spread = dot(hit, results[j][...])
        if side == 0:
            terms = (lane == first) | (lane == first + experts) | (lane == first + 2 * experts)
            column = jnp.where(terms, flat[...], 0.0)
            spread = jnp.sum(column, axis=1, keepdims=True) * spread
        summed = spread if summed is None else summed + spread
    if side == 1:
        summed = gain[...] * summed
    for k in range(blocks):
        part = summed[k * tokens : (k + 1) * tokens]
        if outs[k].dtype == F32:
            outs[k][...] = home[...].astype(F32) + part
        else:
            outs[k][...] = part.astype(BF16)


def combine(packs, results, gain, home, steps, inner, capacity, side):
    packs = [packs[k] for k in steps]
    blocks = len(packs)
    tokens, width = packs[0].shape[0], results[0].shape[1]
    lanes = packs[0].shape[1] - width
    local = shape(tokens, width, dtype=BF16 if side else F32)
    return call(
        functools.partial(combine_kernel, blocks, lanes // 8, inner, capacity, side),
        [shape(tokens, width) if k else local for k in steps],
        (*packs, *results, gain, home),
        COST["combine"],
        scratch=(pltpu.VMEM((blocks * tokens, lanes), F32),),
    )


def output_kernel(*refs):
    total = refs[-2][...]
    for part in refs[:-2]:
        total = total + part[...].astype(F32)
    refs[-1][0] = total.astype(BF16)


def gradient_kernel(*refs):
    home, out = refs[-2:]
    tokens = out.shape[1]
    stream, grad = (home[pl.ds(i * tokens, tokens), :].astype(F32) for i in range(2))
    scale = norm_scale(stream)
    summed = refs[0][...].astype(F32)
    for part in refs[1:-2]:
        summed = summed + part[...].astype(F32)
    inner = jnp.mean(summed * stream, axis=-1, keepdims=True)
    out[0] = (grad + scale * summed - stream * (scale * scale * scale * inner)).astype(BF16)


def on_device(
    fwd_input,
    fwd_routes,
    fwd_gates,
    bwd_input,
    bwd_grad,
    bwd_routes,
    bwd_gates,
    norm_gain,
    w_gate,
    w_up,
    w_down,
):
    experts = lax.axis_size("expert")
    inner = inner_size(experts)
    outer = experts // inner
    tokens, width = fwd_input.shape[1:]
    capacity = min(tokens, tokens * fwd_routes.shape[2] // experts)
    fx, bx, grad = fwd_input[0], bwd_input[0], bwd_grad[0]
    weights = (w_gate[0, 0], w_up[0, 0], w_down[0, 0])

    steps = tuple(range(1, outer))

    def spread(block):
        return [over_outer(block, k, outer, inner) for k in steps]

    def exchanged(blocks, back=False):
        sent = {j: over_inner(blocks[j], j, outer, inner, back) for j in reversed(range(1, inner))}
        return [blocks[0], *(sent[j] for j in range(1, inner))]

    def returned(blocks, steps, distance):
        return [
            home_and_along(block, k, outer, inner, distance) for k, block in zip(steps, blocks)
        ]

    lists = [v[0].T for v in (fwd_routes, fwd_gates, bwd_routes, bwd_gates)]
    f_pack = prepare(experts, *lists, fx, norm_gain)
    b_pack, home, *own = local(f_pack, outer, inner, capacity, bx, grad, norm_gain)
    f_away = spread(f_pack)
    own = exchanged(own)
    every = (*range(outer // 2, outer), *range(1, outer // 2), 0)
    sizes = (width, outer, inner, capacity)
    half = outer // 2
    lower, upper = tuple(range(1, half)), tuple(range(half, outer))
    near = (*lower, 0)
    packs = {0: f_pack, **dict(zip(steps, f_away))}
    b_away = dict(zip(steps, spread(after(b_pack, f_away[0]))))
    f_picked = select(f_away, f_away, *sizes, 0)
    f_rows = exchanged(f_picked)
    f_result = expert(
        forward_kernel, own, f_rows, weights, (every,), steps, capacity, 1, 3, COST["f_expert"]
    )[0]
    f_back = exchanged(f_result, True)

    def b_selected(steps, before):
        chosen = after(([packs[k] for k in steps], [b_away[k] for k in steps]), before)
        return select(*chosen, *sizes, 1)

    def b_expert(rows, steps, given):
        return expert(
            backward_kernel,
            own,
            rows,
            weights,
            (steps,),
            given,
            capacity,
            2,
            5,
            COST["b_expert"],
        )[0]

    def combined(results, steps, home, side):
        return combine(packs, results, norm_gain, home, steps, inner, capacity, side)

    b_low = b_selected(lower, f_result[0])
    b_low_rows = exchanged(b_low)
    b_up = b_selected(upper, (b_low[0], f_back))
    b_up_rows = exchanged(b_up)
    f_sums = combined(after(f_back, b_up[0]), every, fx, 0)
    f_parts = returned(f_sums[: len(upper)], upper, 1)
    low_result = b_expert(after(b_low_rows, f_sums[0]), near, lower)
    f_near, home = after((f_sums[len(upper) :], home), low_result[0])
    f_parts += returned(f_near, near, 1)
    home_next = home_and_along(home, 0, outer, inner, -1)
    up_result = b_expert(after(b_up_rows, (low_result[0], f_parts[0])), upper, upper)
    out = shape(1, tokens, width)
    forward_next = call(output_kernel, out, f_parts, COST["output"])
    up_back = exchanged(up_result, True)
    low_back = exchanged(after(low_result, up_back[1]), True)
    up_sums = combined(after(up_back, (home_next, forward_next)), upper, fx, 1)
    b_parts = returned(up_sums, upper, -1)
    low_sums = combined(after(low_back, up_sums[0]), near, fx, 1)
    b_parts += returned(low_sums, near, -1)
    backward_next = call(gradient_kernel, out, [*b_parts, home_next], COST["gradient"])
    return (forward_next, backward_next)


def solution(mesh):
    placed = (
        P("segment", "expert", None),
        P("segment", "expert", None),
        P("segment", "expert", None),
        P("segment", "expert", None),
        P("segment", "expert", None),
        P("segment", "expert", None),
        P("segment", "expert", None),
        P("segment", None),
        P("segment", "expert", None, None),
        P("segment", "expert", None, None),
        P("segment", "expert", None, None),
    )
    return jax.shard_map(
        on_device,
        mesh=mesh,
        in_specs=placed,
        out_specs=(P("segment", "expert", None), P("segment", "expert", None)),
        check_vma=False,
    )
```

```python
import functools

import jax
import jax.numpy as jnp
from jax import lax
from jax.experimental import pallas as pl
from jax.experimental.pallas import tpu as pltpu
from jax.sharding import PartitionSpec as P

EPSILON = 1e-06
COST = {
    "prepare": 2,
    "local": 2,
    "select": 2,
    "f_expert": 2.25,
    "b_expert": 0.5,
    "combine": 2,
    "output": 2,
    "gradient": 2,
}
BF16 = jnp.bfloat16
F32 = jnp.float32


def inner_size(experts):
    inner = 1
    while inner * inner * 4 <= experts and experts % (inner * 2) == 0:
        inner *= 2
    return inner


def partner(place, step, size, back=False):
    if size & (size - 1) == 0:
        return place ^ step
    return (place + (size - step if back else step)) % size


def over_outer(block, step, outer, inner):
    route = [
        (o * inner + i, partner(o, step, outer) * inner + i)
        for o in range(outer)
        for i in range(inner)
    ]
    return lax.ppermute(block, "expert", route)


def over_inner(block, step, outer, inner, back=False):
    route = [
        (o * inner + i, o * inner + partner(i, step, inner, back))
        for o in range(outer)
        for i in range(inner)
    ]
    return lax.ppermute(block, "expert", route)


def home_and_along(block, step, outer, inner, distance):
    segments = lax.axis_size("segment")
    experts = outer * inner
    route = [
        (
            s * experts + o * inner + i,
            (s + distance) % segments * experts + partner(o, step, outer, True) * inner + i,
        )
        for s in range(segments)
        for o in range(outer)
        for i in range(inner)
    ]
    return lax.ppermute(block, ("segment", "expert"), route)


def after(values, *others):
    return lax.optimization_barrier((values, others))[0]


def norm_scale(stream):
    return lax.rsqrt(jnp.mean(stream * stream, axis=-1, keepdims=True) + EPSILON)


def dot(left, right):
    return jnp.dot(left, right, preferred_element_type=F32)


def dot_nt(left, right):
    return lax.dot_general(left, right, (((1,), (1,)), ((), ())), preferred_element_type=F32)


def call(kernel, out_shape, args, cost, far=(), scratch=(), limit=16 * 2**20):
    near = pl.BlockSpec(memory_space=pltpu.VMEM)
    return pl.pallas_call(
        kernel,
        out_shape=out_shape,
        in_specs=[near] * len(args) + [pl.BlockSpec(memory_space=pltpu.HBM)] * len(far),
        out_specs=jax.tree.map(lambda _: near, out_shape),
        scratch_shapes=[
            *scratch,
            *(pltpu.VMEM(v.shape, v.dtype) for v in far),
            *([pltpu.SemaphoreType.DMA((len(far),))] if far else []),
        ],
        compiler_params=pltpu.CompilerParams(vmem_limit_bytes=limit),
        cost_estimate=pl.CostEstimate(
            flops=int(cost * 2**30), bytes_accessed=2**16, transcendentals=0
        ),
    )(*args, *far)


def fetches(sources, targets, semaphores):
    copies = [
        pltpu.make_async_copy(source, target, semaphores.at[i])
        for i, (source, target) in enumerate(zip(sources, targets))
    ]
    for copy in copies:
        copy.start()
    return copies


def shape(*dims, dtype=BF16):
    return jax.ShapeDtypeStruct(dims, dtype)


def my_expert(step, outer, inner):
    me = lax.axis_index("expert")
    o, i = me // inner, me % inner
    return o * inner + partner(i, step, inner)


def normed_rows(rows, gain):
    stream = rows.astype(F32)
    return (stream * norm_scale(stream) * gain).astype(BF16)


def fill_table(experts, table, lists):
    tokens = table.shape[1]
    row = lax.broadcasted_iota(jnp.int32, (experts, tokens), 0)
    before = lax.broadcasted_iota(jnp.int32, (tokens, tokens), 0) < lax.broadcasted_iota(
        jnp.int32, (tokens, tokens), 1
    )
    before = before.astype(F32).astype(BF16)
    for side, (routes, values) in enumerate((lists[:2], lists[2:])):
        rest = jnp.zeros((experts, tokens), F32)
        chosen = jnp.zeros((experts, tokens), jnp.bool_)
        for k in range(routes.shape[0]):
            here = row == routes[k : k + 1, :]
            rest = jnp.where(here, values[k : k + 1, :], rest)
            chosen = chosen | here
        base = 4 * experts * side
        for term in range(3):
            rounded = rest.astype(BF16).astype(F32)
            table[pl.ds(base + term * experts, experts), :] = rounded
            rest = rest - rounded
        rank = dot(chosen.astype(F32).astype(BF16), before)
        table[pl.ds(base + 3 * experts, experts), :] = jnp.where(chosen, rank, -1.0)


def picked(table, side, expert, experts, blocks, capacity):
    total = table.shape[1]
    shift = lax.broadcasted_iota(jnp.int32, (1, total), 1) // (total // blocks) * capacity
    place = lax.broadcasted_iota(jnp.int32, (blocks * capacity, total), 0)
    rank = table[pl.ds((4 * side + 3) * experts + expert, 1), :].astype(jnp.int32)
    return (jnp.where(rank >= 0, rank + shift, -1) == place).astype(F32)


def gate_of(table, side, expert, experts):
    terms = [table[pl.ds((4 * side + term) * experts + expert, 1), :] for term in range(3)]
    return terms[0] + terms[1] + terms[2]


def all_picked(table, side, outer, inner, blocks, capacity):
    hits, gates = [], []
    for j in range(inner):
        expert = my_expert(j, outer, inner)
        hit = picked(table, side, expert, outer * inner, blocks, capacity)
        gate = gate_of(table, side, expert, outer * inner)
        hits.append(hit)
        gates.append(jnp.sum(hit * gate, axis=1, keepdims=True))
    return jnp.concatenate(hits).astype(BF16), jnp.concatenate(gates)


def prepare_kernel(experts, *refs):
    far, (f_pack,) = refs[:6], refs[6:7]
    table, *near, semaphores = refs[7:]
    copies = fetches(far, near, semaphores)
    lists, (fx, gain) = near[:4], near[4:]
    width = fx.shape[1]
    for copy in copies:
        copy.wait()
    f_pack[:, pl.ds(0, width)] = normed_rows(fx[...], gain[...])
    fill_table(experts, table, lists)
    f_pack[:, pl.ds(width, table.shape[0])] = table[...].T.astype(BF16)


def prepare(experts, *args):
    tokens, width = args[4].shape
    lanes = 8 * experts
    return call(
        functools.partial(prepare_kernel, experts),
        [shape(tokens, width + lanes)],
        (),
        COST["prepare"],
        args,
        scratch=(pltpu.VMEM((lanes, tokens), F32),),
        limit=60 * 2**20,
    )[0]


def local_kernel(outer, inner, capacity, *refs):
    f_pack, far = refs[0], refs[1:4]
    (b_pack, home), own = refs[4:6], refs[6 : 6 + inner]
    table, *near, semaphores = refs[6 + inner :]
    experts = outer * inner
    copies = fetches(far, near, semaphores)
    bx, grad, gain = near
    tokens, width = bx.shape
    table[...] = f_pack[:, pl.ds(width, table.shape[0])].astype(F32).T
    for copy in copies:
        copy.wait()
    b_pack[pl.ds(0, tokens), :] = normed_rows(bx[...], gain[...])
    b_pack[pl.ds(tokens, tokens), :] = grad[...]
    home[pl.ds(0, tokens), :] = bx[...]
    home[pl.ds(tokens, tokens), :] = grad[...]
    f_hits, _ = all_picked(table, 0, outer, inner, 1, capacity)
    b_hits, gates = all_picked(table, 1, outer, inner, 1, capacity)
    f_rows = dot(f_hits, f_pack[:, pl.ds(0, width)]).astype(BF16)
    b_rows = dot(b_hits, b_pack[pl.ds(0, tokens), :]).astype(BF16)
    grads = (gates * dot(b_hits, grad[...])).astype(BF16)
    for part, rows in enumerate((f_rows, b_rows, grads)):
        for j in range(inner):
            own[j][pl.ds(part * capacity, capacity), :] = rows[j * capacity : (j + 1) * capacity]


def local(f_pack, outer, inner, capacity, *args):
    tokens, width = args[0].shape
    lanes = f_pack.shape[1] - width
    return call(
        functools.partial(local_kernel, outer, inner, capacity),
        [shape(2 * tokens, width), shape(2 * tokens, width)]
        + [shape(3 * capacity, width)] * inner,
        (f_pack,),
        COST["local"],
        args,
        scratch=(pltpu.VMEM((lanes, tokens), F32),),
        limit=16 * 2**20,
    )


def select_kernel(outer, inner, capacity, side, blocks, *refs):
    experts = outer * inner
    packs, rows = refs[:blocks], refs[blocks : 2 * blocks]
    outs, (flat, table) = refs[2 * blocks : 2 * blocks + inner], refs[2 * blocks + inner :]
    tokens, width = packs[0].shape[0], flat.shape[1]
    total = blocks * tokens
    for k in range(blocks):
        table[:, pl.ds(k * tokens, tokens)] = packs[k][:, pl.ds(width, 8 * experts)].astype(F32).T
        for part in range(side + 1):
            flat[pl.ds(part * total + k * tokens, tokens), :] = rows[k][
                pl.ds(part * tokens, tokens), pl.ds(0, width)
            ]
    slots = blocks * capacity
    hits, gates = all_picked(table, side, outer, inner, blocks, capacity)
    found = [dot(hits, flat[pl.ds(0, total), :]).astype(BF16)]
    if side == 1:
        found.append((gates * dot(hits, flat[pl.ds(total, total), :])).astype(BF16))
    for part, rows_found in enumerate(found):
        for j in range(inner):
            outs[j][pl.ds(part * slots, slots), :] = rows_found[j * slots : (j + 1) * slots]


def select(packs, rows, width, outer, inner, capacity, side):
    blocks = len(rows)
    tokens = packs[0].shape[0]
    return call(
        functools.partial(select_kernel, outer, inner, capacity, side, blocks),
        [shape(blocks * capacity * (side + 1), width)] * inner,
        (*packs, *rows),
        COST["select"],
        scratch=(
            pltpu.VMEM((blocks * tokens * (side + 1), width), BF16),
            pltpu.VMEM((8 * outer * inner, blocks * tokens), F32),
        ),
    )


def chunks(size, want):
    step = want if size % want == 0 else size
    return [pl.ds(start, step) for start in range(0, size, step)]


def places(inner, groups):
    return [(j, k) for group in groups for j in range(inner) for k in group]


def load_rows(flat, own, others, inner, groups, steps, capacity, part, parts):
    rest = others[0].shape[0] // parts
    first = 0 if parts == 1 else part + 1
    for at, (j, k) in enumerate(places(inner, groups)):
        if k == 0:
            rows = own[j][pl.ds(first * capacity, capacity), :]
        else:
            rows = others[j][pl.ds(part * rest + steps.index(k) * capacity, capacity), :]
        flat[pl.ds(at * capacity, capacity), :] = rows


def store_rows(outs, result, part):
    at = 0
    for out in outs:
        out[:, part] = result[at : at + out.shape[0]]
        at += out.shape[0]


def forward_kernel(inner, groups, steps, capacity, *refs):
    own, others = refs[:inner], refs[inner : 2 * inner]
    w_gate, w_up, w_down = refs[2 * inner : 2 * inner + 3]
    outs, (flat, hidden) = refs[2 * inner + 3 : -2], refs[-2:]
    load_rows(flat, own, others, inner, groups, steps, capacity, 0, 1)
    for part in chunks(w_gate.shape[1], 256):
        gate = dot(flat[...], w_gate[:, part])
        upward = dot(flat[...], w_up[:, part])
        hidden[:, part] = (gate * jax.nn.sigmoid(gate) * upward).astype(BF16)
    for part in chunks(w_down.shape[1], 256):
        store_rows(outs, dot(hidden[...], w_down[:, part]).astype(BF16), part)


def backward_kernel(inner, groups, steps, capacity, *refs):
    own, others = refs[:inner], refs[inner : 2 * inner]
    w_gate, w_up, w_down = refs[2 * inner : 2 * inner + 3]
    outs, (flat, flat_grad, d_gate, d_up) = refs[2 * inner + 3 : -4], refs[-4:]
    load_rows(flat, own, others, inner, groups, steps, capacity, 0, 2)
    load_rows(flat_grad, own, others, inner, groups, steps, capacity, 1, 2)
    for part in chunks(w_gate.shape[1], 256):
        gate = dot(flat[...], w_gate[:, part])
        upward = dot(flat[...], w_up[:, part])
        d_hidden = dot_nt(flat_grad[...], w_down[part, :])
        sigma = jax.nn.sigmoid(gate)
        d_gate[:, part] = (d_hidden * upward * sigma * (1.0 + gate * (1.0 - sigma))).astype(BF16)
        d_up[:, part] = (d_hidden * gate * sigma).astype(BF16)
    for part in chunks(w_gate.shape[0], 256):
        result = dot_nt(d_gate[...], w_gate[part, :]) + dot_nt(d_up[...], w_up[part, :])
        store_rows(outs, result.astype(BF16), part)


def expert(kernel, own, others, weights, groups, steps, capacity, inputs, products, cost):
    inner = len(own)
    count = len(places(inner, groups)) * capacity
    width, hidden = weights[0].shape
    outs = call(
        functools.partial(kernel, inner, groups, steps, capacity),
        [shape(len(group) * capacity, width) for group in groups for _ in range(inner)],
        (*own, *others, *weights),
        scratch=[pltpu.VMEM((count, width), BF16)] * inputs
        + [pltpu.VMEM((count, hidden), BF16)] * inputs,
        cost=cost,
    )
    return [outs[i * inner : (i + 1) * inner] for i in range(len(groups))]


def combine_kernel(blocks, experts, inner, capacity, side, *refs):
    packs, results = refs[:blocks], refs[blocks : blocks + inner]
    gain, home = refs[blocks + inner : blocks + inner + 2]
    outs, flat = refs[blocks + inner + 2 : -1], refs[-1]
    tokens, lanes = packs[0].shape[0], flat.shape[1]
    width = packs[0].shape[1] - lanes
    total = blocks * tokens
    slots = blocks * capacity
    for k in range(blocks):
        flat[pl.ds(k * tokens, tokens), :] = packs[k][:, pl.ds(width, lanes)].astype(F32)
    lane = lax.broadcasted_iota(jnp.int32, (total, lanes), 1)
    shift = lax.broadcasted_iota(jnp.int32, (total, 1), 0) // tokens * capacity
    place = lax.broadcasted_iota(jnp.int32, (total, slots), 1)
    hits, summed = [], None
    for j in range(inner):
        first = 4 * experts * side + my_expert(j, experts // inner, inner)
        column = jnp.where(lane == first + 3 * experts, flat[...], 0.0)
        rank = jnp.sum(column, axis=1, keepdims=True).astype(jnp.int32)
        slot = jnp.where(rank >= 0, rank + shift, -1)
        hit = (slot == place).astype(F32).astype(BF16)
        if side == 1:
            hits.append(hit)
            continue
        spread = dot(hit, results[j][...])
        terms = (lane == first) | (lane == first + experts) | (lane == first + 2 * experts)
        column = jnp.where(terms, flat[...], 0.0)
        spread = jnp.sum(column, axis=1, keepdims=True) * spread
        summed = spread if summed is None else summed + spread
    if side == 1:
        rows = jnp.concatenate([result[...] for result in results])
        summed = gain[...] * dot(jnp.concatenate(hits, axis=1), rows)
    for k in range(blocks):
        part = summed[k * tokens : (k + 1) * tokens]
        if outs[k].dtype == F32:
            outs[k][...] = home[...].astype(F32) + part
        else:
            outs[k][...] = part.astype(BF16)


def combine(packs, results, gain, home, steps, inner, capacity, side):
    packs = [packs[k] for k in steps]
    blocks = len(packs)
    tokens, width = packs[0].shape[0], results[0].shape[1]
    lanes = packs[0].shape[1] - width
    local = shape(tokens, width, dtype=BF16 if side else F32)
    return call(
        functools.partial(combine_kernel, blocks, lanes // 8, inner, capacity, side),
        [shape(tokens, width) if k else local for k in steps],
        (*packs, *results, gain, home),
        COST["combine"],
        scratch=(pltpu.VMEM((blocks * tokens, lanes), F32),),
    )


def output_kernel(*refs):
    total = refs[-2][...]
    for part in refs[:-2]:
        total = total + part[...].astype(F32)
    refs[-1][0] = total.astype(BF16)


def gradient_kernel(*refs):
    home, out = refs[-2:]
    tokens = out.shape[1]
    stream, grad = (home[pl.ds(i * tokens, tokens), :].astype(F32) for i in range(2))
    scale = norm_scale(stream)
    summed = refs[0][...].astype(F32)
    for part in refs[1:-2]:
        summed = summed + part[...].astype(F32)
    inner = jnp.mean(summed * stream, axis=-1, keepdims=True)
    out[0] = (grad + scale * summed - stream * (scale * scale * scale * inner)).astype(BF16)


def on_device(
    fwd_input,
    fwd_routes,
    fwd_gates,
    bwd_input,
    bwd_grad,
    bwd_routes,
    bwd_gates,
    norm_gain,
    w_gate,
    w_up,
    w_down,
):
    experts = lax.axis_size("expert")
    inner = inner_size(experts)
    outer = experts // inner
    tokens, width = fwd_input.shape[1:]
    capacity = min(tokens, tokens * fwd_routes.shape[2] // experts)
    fx, bx, grad = fwd_input[0], bwd_input[0], bwd_grad[0]
    weights = (w_gate[0, 0], w_up[0, 0], w_down[0, 0])

    steps = tuple(range(1, outer))

    def spread(block):
        return [over_outer(block, k, outer, inner) for k in steps]

    def exchanged(blocks, back=False):
        sent = {j: over_inner(blocks[j], j, outer, inner, back) for j in reversed(range(1, inner))}
        return [blocks[0], *(sent[j] for j in range(1, inner))]

    def returned(blocks, steps, distance):
        return [
            home_and_along(block, k, outer, inner, distance) for k, block in zip(steps, blocks)
        ]

    lists = [v[0].T for v in (fwd_routes, fwd_gates, bwd_routes, bwd_gates)]
    f_pack = prepare(experts, *lists, fx, norm_gain)
    b_pack, home, *own = local(f_pack, outer, inner, capacity, bx, grad, norm_gain)
    f_away = spread(f_pack)
    own = exchanged(own)
    every = (*range(outer // 2, outer), *range(1, outer // 2), 0)
    sizes = (width, outer, inner, capacity)
    half = outer // 2
    lower, upper = tuple(range(1, half)), tuple(range(half, outer))
    near = (*lower, 0)
    packs = {0: f_pack, **dict(zip(steps, f_away))}
    b_away = dict(zip(steps, spread(after(b_pack, f_away[0]))))
    f_picked = select(f_away, f_away, *sizes, 0)
    f_rows = exchanged(f_picked)
    f_result = expert(
        forward_kernel, own, f_rows, weights, (every,), steps, capacity, 1, 3, COST["f_expert"]
    )[0]
    f_back = exchanged(f_result, True)

    def b_selected(steps, before):
        chosen = after(([packs[k] for k in steps], [b_away[k] for k in steps]), before)
        return select(*chosen, *sizes, 1)

    def b_expert(rows, steps, given):
        return expert(
            backward_kernel,
            own,
            rows,
            weights,
            (steps,),
            given,
            capacity,
            2,
            5,
            COST["b_expert"],
        )[0]

    def combined(results, steps, home, side):
        return combine(packs, results, norm_gain, home, steps, inner, capacity, side)

    b_low = b_selected(lower, f_picked[0])
    b_low_rows = exchanged(b_low)
    b_up = b_selected(upper, (b_low[0], f_back[:-1]))
    b_up_rows = exchanged(b_up)
    f_sums = combined(after(f_back, b_up[0]), every, fx, 0)
    f_parts = returned(f_sums[: len(upper)], upper, 1)
    low_result = b_expert(after(b_low_rows, f_sums[0]), near, lower)
    f_near, home = after((f_sums[len(upper) :], home), low_result[0])
    f_parts += returned(f_near, near, 1)
    home_next = home_and_along(home, 0, outer, inner, -1)
    up_result = b_expert(after(b_up_rows, (low_result[0], f_parts[0])), upper, upper)
    out = shape(1, tokens, width)
    forward_next = call(output_kernel, out, f_parts, COST["output"])
    up_back = exchanged(up_result, True)
    low_back = exchanged(after(low_result, up_back[1]), True)
    up_sums = combined(after(up_back, (home_next, forward_next)), upper, fx, 1)
    b_parts = returned(up_sums, upper, -1)
    low_sums = combined(after(low_back, up_sums[0]), near, fx, 1)
    b_parts += returned(low_sums, near, -1)
    backward_next = call(gradient_kernel, out, [*b_parts, home_next], COST["gradient"])
    return (forward_next, backward_next)


def solution(mesh):
    placed = (
        P("segment", "expert", None),
        P("segment", "expert", None),
        P("segment", "expert", None),
        P("segment", "expert", None),
        P("segment", "expert", None),
        P("segment", "expert", None),
        P("segment", "expert", None),
        P("segment", None),
        P("segment", "expert", None, None),
        P("segment", "expert", None, None),
        P("segment", "expert", None, None),
    )
    return jax.shard_map(
        on_device,
        mesh=mesh,
        in_specs=placed,
        out_specs=(P("segment", "expert", None), P("segment", "expert", None)),
        check_vma=False,
    )
```

```python
import functools

import jax
import jax.numpy as jnp
from jax import lax
from jax.experimental import pallas as pl
from jax.experimental.pallas import tpu as pltpu
from jax.sharding import PartitionSpec as P

EPSILON = 1e-06
COST = {
    "prepare": 2,
    "local": 2,
    "select": 2,
    "f_expert": 2.25,
    "b_expert": 0.5,
    "combine": 2,
    "output": 2,
    "gradient": 2,
}
BF16 = jnp.bfloat16
F32 = jnp.float32


def inner_size(experts):
    inner = 1
    while inner * inner * 4 <= experts and experts % (inner * 2) == 0:
        inner *= 2
    return inner


def partner(place, step, size, back=False):
    if size & (size - 1) == 0:
        return place ^ step
    return (place + (size - step if back else step)) % size


def over_outer(block, step, outer, inner):
    route = [
        (o * inner + i, partner(o, step, outer) * inner + i)
        for o in range(outer)
        for i in range(inner)
    ]
    return lax.ppermute(block, "expert", route)


def over_inner(block, step, outer, inner, back=False):
    route = [
        (o * inner + i, o * inner + partner(i, step, inner, back))
        for o in range(outer)
        for i in range(inner)
    ]
    return lax.ppermute(block, "expert", route)


def home_and_along(block, step, outer, inner, distance):
    segments = lax.axis_size("segment")
    experts = outer * inner
    route = [
        (
            s * experts + o * inner + i,
            (s + distance) % segments * experts + partner(o, step, outer, True) * inner + i,
        )
        for s in range(segments)
        for o in range(outer)
        for i in range(inner)
    ]
    return lax.ppermute(block, ("segment", "expert"), route)


def after(values, *others):
    return lax.optimization_barrier((values, others))[0]


def norm_scale(stream):
    return lax.rsqrt(jnp.mean(stream * stream, axis=-1, keepdims=True) + EPSILON)


def dot(left, right):
    return jnp.dot(left, right, preferred_element_type=F32)


def dot_nt(left, right):
    return lax.dot_general(left, right, (((1,), (1,)), ((), ())), preferred_element_type=F32)


def call(kernel, out_shape, args, cost, far=(), scratch=(), limit=16 * 2**20):
    near = pl.BlockSpec(memory_space=pltpu.VMEM)
    return pl.pallas_call(
        kernel,
        out_shape=out_shape,
        in_specs=[near] * len(args) + [pl.BlockSpec(memory_space=pltpu.HBM)] * len(far),
        out_specs=jax.tree.map(lambda _: near, out_shape),
        scratch_shapes=[
            *scratch,
            *(pltpu.VMEM(v.shape, v.dtype) for v in far),
            *([pltpu.SemaphoreType.DMA((len(far),))] if far else []),
        ],
        compiler_params=pltpu.CompilerParams(vmem_limit_bytes=limit),
        cost_estimate=pl.CostEstimate(
            flops=int(cost * 2**30), bytes_accessed=2**16, transcendentals=0
        ),
    )(*args, *far)


def fetches(sources, targets, semaphores):
    copies = [
        pltpu.make_async_copy(source, target, semaphores.at[i])
        for i, (source, target) in enumerate(zip(sources, targets))
    ]
    for copy in copies:
        copy.start()
    return copies


def shape(*dims, dtype=BF16):
    return jax.ShapeDtypeStruct(dims, dtype)


def my_expert(step, outer, inner):
    me = lax.axis_index("expert")
    o, i = me // inner, me % inner
    return o * inner + partner(i, step, inner)


def normed_rows(rows, gain):
    stream = rows.astype(F32)
    return (stream * norm_scale(stream) * gain).astype(BF16)


def fill_table(experts, table, lists):
    tokens = table.shape[1]
    row = lax.broadcasted_iota(jnp.int32, (experts, tokens), 0)
    before = lax.broadcasted_iota(jnp.int32, (tokens, tokens), 0) < lax.broadcasted_iota(
        jnp.int32, (tokens, tokens), 1
    )
    before = before.astype(F32).astype(BF16)
    for side, (routes, values) in enumerate((lists[:2], lists[2:])):
        rest = jnp.zeros((experts, tokens), F32)
        chosen = jnp.zeros((experts, tokens), jnp.bool_)
        for k in range(routes.shape[0]):
            here = row == routes[k : k + 1, :]
            rest = jnp.where(here, values[k : k + 1, :], rest)
            chosen = chosen | here
        base = 4 * experts * side
        for term in range(3):
            rounded = rest.astype(BF16).astype(F32)
            table[pl.ds(base + term * experts, experts), :] = rounded
            rest = rest - rounded
        rank = dot(chosen.astype(F32).astype(BF16), before)
        table[pl.ds(base + 3 * experts, experts), :] = jnp.where(chosen, rank, -1.0)


def picked(table, side, expert, experts, blocks, capacity):
    total = table.shape[1]
    shift = lax.broadcasted_iota(jnp.int32, (1, total), 1) // (total // blocks) * capacity
    place = lax.broadcasted_iota(jnp.int32, (blocks * capacity, total), 0)
    rank = table[pl.ds((4 * side + 3) * experts + expert, 1), :].astype(jnp.int32)
    return (jnp.where(rank >= 0, rank + shift, -1) == place).astype(F32)


def gate_of(table, side, expert, experts):
    terms = [table[pl.ds((4 * side + term) * experts + expert, 1), :] for term in range(3)]
    return terms[0] + terms[1] + terms[2]


def all_picked(table, side, outer, inner, blocks, capacity):
    hits, gates = [], []
    for j in range(inner):
        expert = my_expert(j, outer, inner)
        hit = picked(table, side, expert, outer * inner, blocks, capacity)
        gate = gate_of(table, side, expert, outer * inner)
        hits.append(hit)
        gates.append(jnp.sum(hit * gate, axis=1, keepdims=True))
    return jnp.concatenate(hits).astype(BF16), jnp.concatenate(gates)


def prepare_kernel(experts, *refs):
    far, (f_pack,) = refs[:6], refs[6:7]
    table, *near, semaphores = refs[7:]
    copies = fetches(far, near, semaphores)
    lists, (fx, gain) = near[:4], near[4:]
    width = fx.shape[1]
    for copy in copies[4:]:
        copy.wait()
    f_pack[:, pl.ds(0, width)] = normed_rows(fx[...], gain[...])
    for copy in copies[:4]:
        copy.wait()
    fill_table(experts, table, lists)
    f_pack[:, pl.ds(width, table.shape[0])] = table[...].T.astype(BF16)


def prepare(experts, *args):
    tokens, width = args[4].shape
    lanes = 8 * experts
    return call(
        functools.partial(prepare_kernel, experts),
        [shape(tokens, width + lanes)],
        (),
        COST["prepare"],
        args,
        scratch=(pltpu.VMEM((lanes, tokens), F32),),
        limit=60 * 2**20,
    )[0]


def local_kernel(outer, inner, capacity, *refs):
    f_pack, far = refs[0], refs[1:4]
    (b_pack, home), own = refs[4:6], refs[6 : 6 + inner]
    table, *near, semaphores = refs[6 + inner :]
    experts = outer * inner
    copies = fetches(far, near, semaphores)
    bx, grad, gain = near
    tokens, width = bx.shape
    table[...] = f_pack[:, pl.ds(width, table.shape[0])].astype(F32).T
    for copy in copies:
        copy.wait()
    b_pack[pl.ds(0, tokens), :] = normed_rows(bx[...], gain[...])
    b_pack[pl.ds(tokens, tokens), :] = grad[...]
    home[pl.ds(0, tokens), :] = bx[...]
    home[pl.ds(tokens, tokens), :] = grad[...]
    f_hits, _ = all_picked(table, 0, outer, inner, 1, capacity)
    b_hits, gates = all_picked(table, 1, outer, inner, 1, capacity)
    f_rows = dot(f_hits, f_pack[:, pl.ds(0, width)]).astype(BF16)
    b_rows = dot(b_hits, b_pack[pl.ds(0, tokens), :]).astype(BF16)
    grads = (gates * dot(b_hits, grad[...])).astype(BF16)
    for part, rows in enumerate((f_rows, b_rows, grads)):
        for j in range(inner):
            own[j][pl.ds(part * capacity, capacity), :] = rows[j * capacity : (j + 1) * capacity]


def local(f_pack, outer, inner, capacity, *args):
    tokens, width = args[0].shape
    lanes = f_pack.shape[1] - width
    return call(
        functools.partial(local_kernel, outer, inner, capacity),
        [shape(2 * tokens, width), shape(2 * tokens, width)]
        + [shape(3 * capacity, width)] * inner,
        (f_pack,),
        COST["local"],
        args,
        scratch=(pltpu.VMEM((lanes, tokens), F32),),
        limit=16 * 2**20,
    )


def select_kernel(outer, inner, capacity, side, blocks, *refs):
    experts = outer * inner
    packs, rows = refs[:blocks], refs[blocks : 2 * blocks]
    outs, (flat, table) = refs[2 * blocks : 2 * blocks + inner], refs[2 * blocks + inner :]
    tokens, width = packs[0].shape[0], flat.shape[1]
    total = blocks * tokens
    for k in range(blocks):
        table[:, pl.ds(k * tokens, tokens)] = packs[k][:, pl.ds(width, 8 * experts)].astype(F32).T
        for part in range(side + 1):
            flat[pl.ds(part * total + k * tokens, tokens), :] = rows[k][
                pl.ds(part * tokens, tokens), pl.ds(0, width)
            ]
    slots = blocks * capacity
    hits, gates = all_picked(table, side, outer, inner, blocks, capacity)
    found = [dot(hits, flat[pl.ds(0, total), :]).astype(BF16)]
    if side == 1:
        found.append((gates * dot(hits, flat[pl.ds(total, total), :])).astype(BF16))
    for part, rows_found in enumerate(found):
        for j in range(inner):
            outs[j][pl.ds(part * slots, slots), :] = rows_found[j * slots : (j + 1) * slots]


def select(packs, rows, width, outer, inner, capacity, side):
    blocks = len(rows)
    tokens = packs[0].shape[0]
    return call(
        functools.partial(select_kernel, outer, inner, capacity, side, blocks),
        [shape(blocks * capacity * (side + 1), width)] * inner,
        (*packs, *rows),
        COST["select"],
        scratch=(
            pltpu.VMEM((blocks * tokens * (side + 1), width), BF16),
            pltpu.VMEM((8 * outer * inner, blocks * tokens), F32),
        ),
    )


def chunks(size, want):
    step = want if size % want == 0 else size
    return [pl.ds(start, step) for start in range(0, size, step)]


def places(inner, groups):
    return [(j, k) for group in groups for j in range(inner) for k in group]


def load_rows(flat, own, others, inner, groups, steps, capacity, part, parts):
    rest = others[0].shape[0] // parts
    first = 0 if parts == 1 else part + 1
    for at, (j, k) in enumerate(places(inner, groups)):
        if k == 0:
            rows = own[j][pl.ds(first * capacity, capacity), :]
        else:
            rows = others[j][pl.ds(part * rest + steps.index(k) * capacity, capacity), :]
        flat[pl.ds(at * capacity, capacity), :] = rows


def store_rows(outs, result, part):
    at = 0
    for out in outs:
        out[:, part] = result[at : at + out.shape[0]]
        at += out.shape[0]


def forward_kernel(inner, groups, steps, capacity, *refs):
    own, others = refs[:inner], refs[inner : 2 * inner]
    w_gate, w_up, w_down = refs[2 * inner : 2 * inner + 3]
    outs, (flat, hidden) = refs[2 * inner + 3 : -2], refs[-2:]
    load_rows(flat, own, others, inner, groups, steps, capacity, 0, 1)
    for part in chunks(w_gate.shape[1], 256):
        gate = dot(flat[...], w_gate[:, part])
        upward = dot(flat[...], w_up[:, part])
        hidden[:, part] = (gate * jax.nn.sigmoid(gate) * upward).astype(BF16)
    for part in chunks(w_down.shape[1], 256):
        store_rows(outs, dot(hidden[...], w_down[:, part]).astype(BF16), part)


def backward_kernel(inner, groups, steps, capacity, *refs):
    own, others = refs[:inner], refs[inner : 2 * inner]
    w_gate, w_up, w_down = refs[2 * inner : 2 * inner + 3]
    outs, (flat, flat_grad, d_gate, d_up) = refs[2 * inner + 3 : -4], refs[-4:]
    load_rows(flat, own, others, inner, groups, steps, capacity, 0, 2)
    load_rows(flat_grad, own, others, inner, groups, steps, capacity, 1, 2)
    for part in chunks(w_gate.shape[1], 256):
        gate = dot(flat[...], w_gate[:, part])
        upward = dot(flat[...], w_up[:, part])
        d_hidden = dot_nt(flat_grad[...], w_down[part, :])
        sigma = jax.nn.sigmoid(gate)
        d_gate[:, part] = (d_hidden * upward * sigma * (1.0 + gate * (1.0 - sigma))).astype(BF16)
        d_up[:, part] = (d_hidden * gate * sigma).astype(BF16)
    for part in chunks(w_gate.shape[0], 256):
        result = dot_nt(d_gate[...], w_gate[part, :]) + dot_nt(d_up[...], w_up[part, :])
        store_rows(outs, result.astype(BF16), part)


def expert(kernel, own, others, weights, groups, steps, capacity, inputs, products, cost):
    inner = len(own)
    count = len(places(inner, groups)) * capacity
    width, hidden = weights[0].shape
    outs = call(
        functools.partial(kernel, inner, groups, steps, capacity),
        [shape(len(group) * capacity, width) for group in groups for _ in range(inner)],
        (*own, *others, *weights),
        scratch=[pltpu.VMEM((count, width), BF16)] * inputs
        + [pltpu.VMEM((count, hidden), BF16)] * inputs,
        cost=cost,
    )
    return [outs[i * inner : (i + 1) * inner] for i in range(len(groups))]


def combine_kernel(blocks, experts, inner, capacity, side, *refs):
    packs, results = refs[:blocks], refs[blocks : blocks + inner]
    gain, home = refs[blocks + inner : blocks + inner + 2]
    outs, flat = refs[blocks + inner + 2 : -1], refs[-1]
    tokens, lanes = packs[0].shape[0], flat.shape[1]
    width = packs[0].shape[1] - lanes
    total = blocks * tokens
    slots = blocks * capacity
    for k in range(blocks):
        flat[pl.ds(k * tokens, tokens), :] = packs[k][:, pl.ds(width, lanes)].astype(F32)
    lane = lax.broadcasted_iota(jnp.int32, (total, lanes), 1)
    shift = lax.broadcasted_iota(jnp.int32, (total, 1), 0) // tokens * capacity
    place = lax.broadcasted_iota(jnp.int32, (total, slots), 1)
    hits, summed = [], None
    for j in range(inner):
        first = 4 * experts * side + my_expert(j, experts // inner, inner)
        column = jnp.where(lane == first + 3 * experts, flat[...], 0.0)
        rank = jnp.sum(column, axis=1, keepdims=True).astype(jnp.int32)
        slot = jnp.where(rank >= 0, rank + shift, -1)
        hit = (slot == place).astype(F32).astype(BF16)
        if side == 1:
            hits.append(hit)
            continue
        spread = dot(hit, results[j][...])
        terms = (lane == first) | (lane == first + experts) | (lane == first + 2 * experts)
        column = jnp.where(terms, flat[...], 0.0)
        spread = jnp.sum(column, axis=1, keepdims=True) * spread
        summed = spread if summed is None else summed + spread
    if side == 1:
        rows = jnp.concatenate([result[...] for result in results])
        summed = gain[...] * dot(jnp.concatenate(hits, axis=1), rows)
    for k in range(blocks):
        part = summed[k * tokens : (k + 1) * tokens]
        if outs[k].dtype == F32:
            outs[k][...] = home[...].astype(F32) + part
        else:
            outs[k][...] = part.astype(BF16)


def combine(packs, results, gain, home, steps, inner, capacity, side):
    packs = [packs[k] for k in steps]
    blocks = len(packs)
    tokens, width = packs[0].shape[0], results[0].shape[1]
    lanes = packs[0].shape[1] - width
    local = shape(tokens, width, dtype=BF16 if side else F32)
    return call(
        functools.partial(combine_kernel, blocks, lanes // 8, inner, capacity, side),
        [shape(tokens, width) if k else local for k in steps],
        (*packs, *results, gain, home),
        COST["combine"],
        scratch=(pltpu.VMEM((blocks * tokens, lanes), F32),),
    )


def output_kernel(*refs):
    total = refs[-2][...]
    for part in refs[:-2]:
        total = total + part[...].astype(F32)
    refs[-1][0] = total.astype(BF16)


def gradient_kernel(*refs):
    home, out = refs[-2:]
    tokens = out.shape[1]
    stream, grad = (home[pl.ds(i * tokens, tokens), :].astype(F32) for i in range(2))
    scale = norm_scale(stream)
    summed = refs[0][...].astype(F32)
    for part in refs[1:-2]:
        summed = summed + part[...].astype(F32)
    inner = jnp.mean(summed * stream, axis=-1, keepdims=True)
    out[0] = (grad + scale * summed - stream * (scale * scale * scale * inner)).astype(BF16)


def on_device(
    fwd_input,
    fwd_routes,
    fwd_gates,
    bwd_input,
    bwd_grad,
    bwd_routes,
    bwd_gates,
    norm_gain,
    w_gate,
    w_up,
    w_down,
):
    experts = lax.axis_size("expert")
    inner = inner_size(experts)
    outer = experts // inner
    tokens, width = fwd_input.shape[1:]
    capacity = min(tokens, tokens * fwd_routes.shape[2] // experts)
    fx, bx, grad = fwd_input[0], bwd_input[0], bwd_grad[0]
    weights = (w_gate[0, 0], w_up[0, 0], w_down[0, 0])

    steps = tuple(range(1, outer))

    def spread(block):
        return [over_outer(block, k, outer, inner) for k in steps]

    def exchanged(blocks, back=False):
        sent = {j: over_inner(blocks[j], j, outer, inner, back) for j in reversed(range(1, inner))}
        return [blocks[0], *(sent[j] for j in range(1, inner))]

    def returned(blocks, steps, distance):
        return [
            home_and_along(block, k, outer, inner, distance) for k, block in zip(steps, blocks)
        ]

    lists = [v[0].T for v in (fwd_routes, fwd_gates, bwd_routes, bwd_gates)]
    f_pack = prepare(experts, *lists, fx, norm_gain)
    b_pack, home, *own = local(f_pack, outer, inner, capacity, bx, grad, norm_gain)
    f_away = spread(f_pack)
    own = exchanged(own)
    every = (*range(outer // 2, outer), *range(1, outer // 2), 0)
    sizes = (width, outer, inner, capacity)
    half = outer // 2
    lower, upper = tuple(range(1, half)), tuple(range(half, outer))
    near = (*lower, 0)
    packs = {0: f_pack, **dict(zip(steps, f_away))}
    b_away = dict(zip(steps, spread(after(b_pack, f_away[0]))))
    f_picked = select(f_away, f_away, *sizes, 0)
    f_rows = exchanged(f_picked)
    f_result = expert(
        forward_kernel, own, f_rows, weights, (every,), steps, capacity, 1, 3, COST["f_expert"]
    )[0]
    f_back = exchanged(f_result, True)

    def b_selected(steps, before):
        chosen = after(([packs[k] for k in steps], [b_away[k] for k in steps]), before)
        return select(*chosen, *sizes, 1)

    def b_expert(rows, steps, given):
        return expert(
            backward_kernel,
            own,
            rows,
            weights,
            (steps,),
            given,
            capacity,
            2,
            5,
            COST["b_expert"],
        )[0]

    def combined(results, steps, home, side):
        return combine(packs, results, norm_gain, home, steps, inner, capacity, side)

    b_low = b_selected(lower, f_picked[0])
    b_low_rows = exchanged(b_low)
    b_up = b_selected(upper, (b_low[0], f_back[:-1]))
    b_up_rows = exchanged(b_up)
    f_sums = combined(after(f_back, b_up[0]), every, fx, 0)
    f_parts = returned(f_sums[: len(upper)], upper, 1)
    low_result = b_expert(after(b_low_rows, f_sums[0]), near, lower)
    f_near, home = after((f_sums[len(upper) :], home), low_result[0])
    f_parts += returned(f_near, near, 1)
    home_next = home_and_along(home, 0, outer, inner, -1)
    up_result = b_expert(after(b_up_rows, (low_result[0], f_parts[0])), upper, upper)
    out = shape(1, tokens, width)
    forward_next = call(output_kernel, out, f_parts, COST["output"])
    up_back = exchanged(up_result, True)
    low_back = exchanged(after(low_result, up_back[1]), True)
    up_sums = combined(after(up_back, (home_next, forward_next)), upper, fx, 1)
    b_parts = returned(up_sums, upper, -1)
    low_sums = combined(after(low_back, up_sums[0]), near, fx, 1)
    b_parts += returned(low_sums, near, -1)
    backward_next = call(gradient_kernel, out, [*b_parts, home_next], COST["gradient"])
    return (forward_next, backward_next)


def solution(mesh):
    placed = (
        P("segment", "expert", None),
        P("segment", "expert", None),
        P("segment", "expert", None),
        P("segment", "expert", None),
        P("segment", "expert", None),
        P("segment", "expert", None),
        P("segment", "expert", None),
        P("segment", None),
        P("segment", "expert", None, None),
        P("segment", "expert", None, None),
        P("segment", "expert", None, None),
    )
    return jax.shard_map(
        on_device,
        mesh=mesh,
        in_specs=placed,
        out_specs=(P("segment", "expert", None), P("segment", "expert", None)),
        check_vma=False,
    )
```
